32 devices in a mesh: grp: 2 (over x), row: 16 (over z, y, core).
Axes of the slice: x: 2, y: 2, z: 4, core: 2. Of those that a mesh axis runs over, the one named last changes fastest.
Arguments:
- three_index: bfloat16 [4, 4096, 2048], P(None, 'row', 'grp'), parts along dimension 2, may hold values from -6 to 6
- occupied_factor: bfloat16 [128, 64, 64], P('grp'), parts along dimension 0, may hold values from -0.75 to 0.75
- virtual_factor: bfloat16 [128, 64, 64], P('grp'), parts along dimension 0, may hold values from -0.75 to 0.75
- pair_list: int32 [32, 4], P('grp'), parts along dimension 0, may hold values from 0 to 15, as said below
- occupancy: int32 [32], P('grp'), parts along dimension 0, may hold values from 2 to 4, as said below
- pair_blocks: int32 [16, 2], replicated, may hold values from 0 to 63
Outputs:
- polar_band: float32 [2048, 320], P(('grp', 'row')), parts along dimension 0
The draws below stay inside these ranges and needn't reach their ends.
There are 2 independent parts, one for each index of `grp`. The reference program is written for one: setup_inputs(seed, part) draws one part's arguments, and reference() takes and returns one part's arrays. A program takes and returns all parts, laid end to end along the dimension named above; an argument that names none is the same for every part. Nothing has to cross between parts.
Inputs may be any that keep to these rules, and one draw needn't show every extreme that they name: `pair_list`: row g holds 4 distinct values, each (g + t) mod 16 for some t from 0 to 4. `occupancy`: some group is fully occupied.
All inputs are finite; a program needn't handle non-finite values.
Results may differ from the reference program's by a relative error of at most 0.00082.
Values may be sent and summed in bfloat16 or wider, within the bound.
No kernel may reach another device: no remote copies, remote signals or barrier semaphores. Data moves between devices by JAX's collectives and lax.ppermute only.
A program may use at most 64 MiB of HBM per device.

```python
import jax
import jax.numpy as jnp
from jax import lax

TILE = 64
REACH = 2
SLOTS = 4
AUX_DEV = 64
NBLK = 64
AUX = 1024
NPAIR = 16
BAND = 5
N_ROW = 16


def draw_pair_list(key, part):
    key = jax.random.fold_in(key, 11)
    subkeys = jax.random.split(key, N_ROW)
    offsets = jax.vmap(lambda single: jax.random.permutation(single, SLOTS + 1))(subkeys)[:, :SLOTS]
    groups = jnp.arange(N_ROW, dtype=jnp.int32)[:, None]
    return ((groups + offsets.astype(jnp.int32)) % N_ROW).astype(jnp.int32)


def draw_occupancy(key, part):
    key = jax.random.fold_in(key, 23)
    first_key, second_key = jax.random.split(key)
    counts = jax.random.randint(first_key, (N_ROW,), 2, SLOTS + 1)
    chosen = jax.random.randint(second_key, (), 0, N_ROW)
    return jnp.where(jnp.arange(N_ROW) == chosen, SLOTS, counts).astype(jnp.int32)


def plant(drawn, key, low, largest):
    dims = drawn.shape
    index_at = [jax.random.randint(jax.random.fold_in(key, axis), (), 0, dims[axis]) for axis in range(len(dims))]
    drawn = drawn.at[tuple(index_at)].set(low)
    longest = dims.index(max(dims))
    index_at[longest] = (index_at[longest] + 1) % dims[longest]
    return drawn.at[tuple(index_at)].set(largest)


def levels(stream_key, dims, cuts, smallest, high):
    level = 1.0
    for dim, shards_of in cuts:
        steps = jax.random.uniform(jax.random.fold_in(jax.random.fold_in(stream_key, 6), dim), (shards_of,), jnp.float32, smallest / len(cuts), high / len(cuts))
        level = level * jnp.repeat(jnp.exp(steps), dims[dim] // shards_of).reshape((-1,) + (1,) * (len(dims) - 1 - dim))
    return level


def normal_values(rng, extent, deviation, reach, cuts=(), held_as=jnp.bfloat16):
    entries = deviation * jax.random.normal(rng, extent, jnp.float32)
    if cuts:
        entries = entries * levels(rng, extent, cuts, -0.22, 0.18)
    return jnp.clip(entries, -reach, reach).astype(held_as)


def setup_inputs(seed: int = 0, part: int = 0) -> dict:
    arg_keys = jax.random.split(jax.random.key(seed), 7)
    part_keys = jax.random.split(jax.random.fold_in(arg_keys[6], part), 7)
    return {
        "three_index": normal_values(part_keys[0], (SLOTS, TILE * TILE, AUX), 1.0, 6.0, ((1, 16),)),
        "occupied_factor": normal_values(part_keys[1], (NBLK, TILE, TILE), TILE ** -0.5, 0.75),
        "virtual_factor": normal_values(part_keys[2], (NBLK, TILE, TILE), TILE ** -0.5, 0.75),
        "pair_list": draw_pair_list(jax.random.fold_in(jax.random.fold_in(arg_keys[6], part), 71), part),
        "occupancy": draw_occupancy(jax.random.fold_in(jax.random.fold_in(arg_keys[6], part), 71), part),
        "pair_blocks": plant(jax.random.randint(arg_keys[5], (NPAIR, 2), 0, NBLK), jax.random.fold_in(arg_keys[5], 1), 0, NBLK - 1).astype(jnp.int32),
    }


def transform(block_tiles, listed, occupied_factor, virtual_factor, pair_blocks):
    rows_of = pair_blocks[listed, 0]
    cols_of = pair_blocks[listed, 1]
    left = occupied_factor[rows_of].astype(jnp.float32)
    right = virtual_factor[cols_of].astype(jnp.float32)
    tiles = block_tiles.astype(jnp.float32).reshape(AUX_DEV, SLOTS, TILE, TILE)
    half = jnp.einsum('psmn,snq->psmq', tiles, right).astype(jnp.bfloat16)
    folded = jnp.einsum('sma,psmq->psaq', left, half.astype(jnp.float32)).astype(jnp.bfloat16)
    return folded.reshape(AUX_DEV, SLOTS, TILE * TILE)


def reference(three_index, occupied_factor, virtual_factor, pair_list, occupancy, pair_blocks):
    by_function = jnp.transpose(three_index, (2, 0, 1))
    grouped = by_function.reshape(N_ROW, AUX_DEV, SLOTS, TILE * TILE)

    def make_panel(inputs):
        return transform(inputs[0], inputs[1], occupied_factor, virtual_factor, pair_blocks)

    panels = lax.map(make_panel, (grouped, pair_list))
    slot_index = jnp.arange(SLOTS, dtype=jnp.int32)

    def one_group(group):
        own = panels[group].reshape(AUX_DEV, SLOTS * TILE * TILE)
        own_list = pair_list[group]
        own_valid = slot_index < occupancy[group]
        columns = []
        for offset in range(-REACH, REACH + 1):
            other = ((group + offset) % N_ROW).astype(jnp.int32)
            other_valid = slot_index < occupancy[other]
            match = (own_list[:, None] == pair_list[other][None, :]) & own_valid[:, None] & other_valid[None, :]
            aligned = jnp.einsum('ij,qjx->qix', match.astype(jnp.float32), panels[other].astype(jnp.float32)).astype(jnp.bfloat16)
            block = jnp.dot(own, aligned.reshape(AUX_DEV, SLOTS * TILE * TILE).T, preferred_element_type=jnp.float32)
            columns.append(block)
        return jnp.concatenate(columns, axis=1) * (0.5 / TILE)

    band = lax.map(one_group, jnp.arange(N_ROW, dtype=jnp.int32))
    return band.reshape(AUX, BAND * AUX_DEV)
```

```python
import functools

import jax
import jax.numpy as jnp
from jax import lax
from jax.experimental import pallas as pl
from jax.experimental.pallas import tpu as pltpu
from jax.sharding import PartitionSpec as P

TILE = 64
SPAN = 5
REACH = 2
LANES = 128
ROWS = 256
FOLD = ROWS // TILE


def pack_kernel(list_ref, occupancy_ref, source_ref, packed_ref):
    count, slots = list_ref.shape
    entries = source_ref.shape[1]
    low_half = lax.broadcasted_iota(jnp.int32, (1, LANES), 1) < TILE

    def pick(group, pair):
        slot = jnp.int32(0)
        found = jnp.int32(0)
        for j in range(slots):
            hit = (list_ref[group, j] == pair) & (j < occupancy_ref[group])
            slot = jnp.where(hit, j, slot)
            found = jnp.where(hit, 1, found)
        return slot, found

    def columns(group):
        return pl.ds(pl.multiple_of((group // 2) * LANES, LANES), LANES)

    def step(index, carry):
        for parity in range(2):
            pair = 2 * index + parity
            for couple in range(2):
                first = lax.rem(pair - 4 + 2 * couple + count, count)
                second = lax.rem(pair - 3 + 2 * couple + count, count)
                low, high = (first, second) if parity == 0 else (second, first)
                low_slot, low_found = pick(low, pair)
                high_slot, high_found = pick(high, pair)
                found = jnp.where(low_half, low_found, high_found) > 0
                value = jnp.where(
                    low_half,
                    source_ref[low_slot, :, columns(low)],
                    source_ref[high_slot, :, columns(high)],
                )
                packed_ref[pair, pl.ds(couple * entries, entries), :] = jnp.where(
                    found, value, jnp.zeros_like(value)
                )
            slot, found = pick(pair, pair)
            value = source_ref[slot, :, columns(pair)]
            value = jnp.where(found > 0, value, jnp.zeros_like(value))
            upper, under = value[: entries // 2], value[entries // 2 :]
            if parity == 0:
                folded = jnp.concatenate([upper[:, :TILE], under[:, :TILE]], axis=1)
            else:
                folded = jnp.concatenate([upper[:, TILE:], under[:, TILE:]], axis=1)
            packed_ref[pair, pl.ds(2 * entries, entries // 2), :] = folded
        return carry

    lax.fori_loop(0, count // 2, step, 0)


def pack(three_index, pair_list, occupancy):
    count = pair_list.shape[0]
    entries = three_index.shape[1]
    return pl.pallas_call(
        pack_kernel,
        out_shape=jax.ShapeDtypeStruct((count, 5 * entries // 2, LANES), jnp.bfloat16),
        in_specs=[
            pl.BlockSpec(memory_space=pltpu.SMEM),
            pl.BlockSpec(memory_space=pltpu.SMEM),
            pl.BlockSpec(memory_space=pltpu.VMEM),
        ],
        out_specs=pl.BlockSpec(memory_space=pltpu.VMEM),
        compiler_params=pltpu.CompilerParams(vmem_limit_bytes=32 * 1024 * 1024),
        name="pack",
    )(pair_list, occupancy, three_index)


def factor_kernel(index_ref, occupied_ref, virtual_ref, left_ref, right_ref):
    row = lax.broadcasted_iota(jnp.int32, (ROWS, ROWS), 0)
    column = lax.broadcasted_iota(jnp.int32, (ROWS, ROWS), 1)
    spread = (
        lax.broadcasted_iota(jnp.int32, (ROWS, TILE), 0) // FOLD
        == lax.broadcasted_iota(jnp.int32, (ROWS, TILE), 1)
    ).astype(jnp.bfloat16)
    block = lax.dot_general(
        spread, virtual_ref[0], (((1,), (1,)), ((), ())), preferred_element_type=jnp.float32
    )
    block = jnp.concatenate([block] * FOLD, axis=1)
    right_ref[...] = jnp.where(row % FOLD == column // TILE, block, 0.0).astype(jnp.bfloat16)
    entry = lax.broadcasted_iota(jnp.int32, (TILE, ROWS), 1)
    spread = (
        (entry // (FOLD * FOLD)) * FOLD + entry % FOLD
        == lax.broadcasted_iota(jnp.int32, (TILE, ROWS), 0)
    ).astype(jnp.bfloat16)
    block = lax.dot_general(
        occupied_ref[0], spread, (((0,), (0,)), ((), ())), preferred_element_type=jnp.float32
    )
    block = jnp.concatenate([block] * FOLD, axis=0)
    left_ref[...] = jnp.where(row // TILE == (column // FOLD) % FOLD, block, 0.0).astype(
        jnp.bfloat16
    )


def factors(blocks, occupied_factor, virtual_factor):
    shape = jax.ShapeDtypeStruct((ROWS, ROWS), jnp.bfloat16)
    whole = pl.BlockSpec((ROWS, ROWS), lambda i, index: (0, 0))
    return pl.pallas_call(
        factor_kernel,
        out_shape=(shape, shape),
        grid_spec=pltpu.PrefetchScalarGridSpec(
            num_scalar_prefetch=1,
            grid=(1,),
            in_specs=[
                pl.BlockSpec((1, TILE, TILE), lambda i, index: (index[0], 0, 0)),
                pl.BlockSpec((1, TILE, TILE), lambda i, index: (index[1], 0, 0)),
            ],
            out_specs=(whole, whole),
        ),
        cost_estimate=pl.CostEstimate(
            flops=4_000_000, bytes_accessed=300_000, transcendentals=0
        ),
        name="factors",
    )(blocks, occupied_factor, virtual_factor)


def gram_kernel(parity_ref, left_ref, right_ref, tiles_ref, *refs):
    outs, half_ref, gram_ref = refs[:SPAN], refs[SPAN], refs[SPAN + 1]
    entries = tiles_ref.shape[1] * 2 // 5
    sources = ROWS // entries
    steps = ROWS // (FOLD * FOLD)
    for block in range(TILE * TILE // ROWS):
        span = pl.ds(block * sources, sources)
        first = tiles_ref[span, pl.ds(0, entries), :].reshape(ROWS, LANES)
        second = tiles_ref[span, pl.ds(entries, entries), :].reshape(ROWS, LANES)
        third = tiles_ref[span, pl.ds(2 * entries, entries // 2), :]
        third = jnp.concatenate([third[..., :TILE], third[..., TILE:]], axis=1)
        values = jnp.concatenate([first, second, third.reshape(ROWS, TILE)], axis=1)
        half = jnp.dot(right_ref[...], values, preferred_element_type=jnp.float32)
        half_ref[block] = half.astype(jnp.bfloat16).reshape(steps, FOLD * FOLD, SPAN * TILE)
    for step in range(steps):
        values = half_ref[:, step].reshape(ROWS, SPAN * TILE)
        panel = jnp.dot(left_ref[...], values, preferred_element_type=jnp.float32)
        panel = panel.astype(jnp.bfloat16)
        part = lax.dot_general(
            panel, panel, (((0,), (0,)), ((), ())), preferred_element_type=jnp.float32
        )
        if step == 0:
            gram_ref[...] = part
        else:
            gram_ref[...] += part
    odd = parity_ref[0] == 1
    scale = 0.5 / TILE
    for place in range(SPAN):
        swapped = place ^ 1 if place < SPAN - 1 else place
        rows = jnp.where(
            odd,
            gram_ref[pl.ds(swapped * TILE, TILE), :],
            gram_ref[pl.ds(place * TILE, TILE), :],
        )
        rows = rows * scale
        pieces = []
        for other in range(max(place - REACH, 0), min(place + REACH, SPAN - 1) + 1):
            turned = other ^ 1 if other < SPAN - 1 else other
            pieces.append(
                jnp.where(
                    odd,
                    rows[:, turned * TILE : (turned + 1) * TILE],
                    rows[:, other * TILE : (other + 1) * TILE],
                )
            )
        outs[place][...] = jnp.concatenate(pieces, axis=1)


def neighbours(place):
    return min(place + REACH, SPAN - 1) - max(place - REACH, 0) + 1


def gram(parity, left, right, tiles):
    vmem = pl.BlockSpec(memory_space=pltpu.VMEM)
    return pl.pallas_call(
        gram_kernel,
        out_shape=tuple(
            jax.ShapeDtypeStruct((TILE, TILE * neighbours(place)), jnp.float32)
            for place in range(SPAN)
        ),
        in_specs=[pl.BlockSpec(memory_space=pltpu.SMEM), vmem, vmem, vmem],
        out_specs=(vmem,) * SPAN,
        scratch_shapes=[
            pltpu.VMEM((TILE * TILE // ROWS, ROWS // (FOLD * FOLD), FOLD * FOLD, SPAN * TILE), jnp.bfloat16),
            pltpu.VMEM((SPAN * TILE, SPAN * TILE), jnp.float32),
        ],
        compiler_params=pltpu.CompilerParams(vmem_limit_bytes=32 * 1024 * 1024),
        name="gram",
    )(parity, left, right, tiles)


def local(three_index, occupied_factor, virtual_factor, pair_list, occupancy, pair_blocks):
    count = lax.axis_size("row")
    own = lax.axis_index("row")
    packed = pack(three_index, pair_list, occupancy)
    tiles = lax.all_to_all(packed, "row", split_axis=0, concat_axis=0, tiled=True)
    blocks = lax.dynamic_index_in_dim(pair_blocks, own, 0, keepdims=False)
    left, right = factors(blocks, occupied_factor, virtual_factor)
    parity = lax.rem(own, 2).reshape(1).astype(jnp.int32)
    parts = gram(parity, left, right, tiles)
    total = None
    for place in range(SPAN):
        behind = SPAN - 1 - place
        part = parts[place]
        if behind:
            part = lax.ppermute(
                part, "row", [(source, (source - behind) % count) for source in range(count)]
            )
        before = max(REACH - place, 0) * TILE
        after = (2 * REACH + 1) * TILE - before - part.shape[1]
        part = jnp.pad(part, ((0, 0), (before, after)))
        total = part if total is None else total + part
    return total


def solution(mesh):
    placed = (
        P(None, "row", "grp"),
        P("grp", None, None),
        P("grp", None, None),
        P("grp", None),
        P("grp"),
        P(),
    )
    return jax.shard_map(
        local, mesh=mesh, in_specs=placed, out_specs=P(("grp", "row"), None), check_vma=False
    )
```

```python
import functools

import jax
import jax.numpy as jnp
from jax import lax
from jax.experimental import pallas as pl
from jax.experimental.pallas import tpu as pltpu
from jax.sharding import PartitionSpec as P

TILE = 64
SPAN = 5
REACH = 2
LANES = 128
ROWS = 256
FOLD = ROWS // TILE


def pack_kernel(list_ref, occupancy_ref, source_ref, packed_ref):
    count, slots = list_ref.shape
    entries = source_ref.shape[1]
    low_half = lax.broadcasted_iota(jnp.int32, (1, LANES), 1) < TILE

    def pick(group, pair):
        slot = jnp.int32(0)
        found = jnp.int32(0)
        for j in range(slots):
            hit = (list_ref[group, j] == pair) & (j < occupancy_ref[group])
            slot = jnp.where(hit, j, slot)
            found = jnp.where(hit, 1, found)
        return slot, found

    def columns(group):
        return pl.ds(pl.multiple_of((group // 2) * LANES, LANES), LANES)

    def step(index, carry):
        for parity in range(2):
            pair = 2 * index + parity
            for couple in range(2):
                first = lax.rem(pair - 4 + 2 * couple + count, count)
                second = lax.rem(pair - 3 + 2 * couple + count, count)
                low, high = (first, second) if parity == 0 else (second, first)
                low_slot, low_found = pick(low, pair)
                high_slot, high_found = pick(high, pair)
                found = jnp.where(low_half, low_found, high_found) > 0
                value = jnp.where(
                    low_half,
                    source_ref[low_slot, :, columns(low)],
                    source_ref[high_slot, :, columns(high)],
                )
                packed_ref[pair, pl.ds(couple * entries, entries), :] = jnp.where(
                    found, value, jnp.zeros_like(value)
                )
            slot, found = pick(pair, pair)
            value = source_ref[slot, :, columns(pair)]
            value = jnp.where(found > 0, value, jnp.zeros_like(value))
            upper, under = value[: entries // 2], value[entries // 2 :]
            if parity == 0:
                folded = jnp.concatenate([upper[:, :TILE], under[:, :TILE]], axis=1)
            else:
                folded = jnp.concatenate([upper[:, TILE:], under[:, TILE:]], axis=1)
            packed_ref[pair, pl.ds(2 * entries, entries // 2), :] = folded
        return carry

    lax.fori_loop(0, count // 2, step, 0)


def pack(three_index, pair_list, occupancy):
    count = pair_list.shape[0]
    entries = three_index.shape[1]
    return pl.pallas_call(
        pack_kernel,
        out_shape=jax.ShapeDtypeStruct((count, 5 * entries // 2, LANES), jnp.bfloat16),
        in_specs=[
            pl.BlockSpec(memory_space=pltpu.SMEM),
            pl.BlockSpec(memory_space=pltpu.SMEM),
            pl.BlockSpec(memory_space=pltpu.VMEM),
        ],
        out_specs=pl.BlockSpec(memory_space=pltpu.VMEM),
        compiler_params=pltpu.CompilerParams(vmem_limit_bytes=32 * 1024 * 1024),
        name="pack",
    )(pair_list, occupancy, three_index)


def factor_kernel(index_ref, occupied_ref, virtual_ref, left_ref, right_ref):
    row = lax.broadcasted_iota(jnp.int32, (ROWS, ROWS), 0)
    column = lax.broadcasted_iota(jnp.int32, (ROWS, ROWS), 1)
    spread = (
        lax.broadcasted_iota(jnp.int32, (ROWS, TILE), 0) // FOLD
        == lax.broadcasted_iota(jnp.int32, (ROWS, TILE), 1)
    ).astype(jnp.bfloat16)
    block = lax.dot_general(
        spread, virtual_ref[0], (((1,), (1,)), ((), ())), preferred_element_type=jnp.float32
    )
    block = jnp.concatenate([block] * FOLD, axis=1)
    right_ref[...] = jnp.where(row % FOLD == column // TILE, block, 0.0).astype(jnp.bfloat16)
    entry = lax.broadcasted_iota(jnp.int32, (TILE, ROWS), 1)
    spread = (
        (entry // (FOLD * FOLD)) * FOLD + entry % FOLD
        == lax.broadcasted_iota(jnp.int32, (TILE, ROWS), 0)
    ).astype(jnp.bfloat16)
    block = lax.dot_general(
        occupied_ref[0], spread, (((0,), (0,)), ((), ())), preferred_element_type=jnp.float32
    )
    block = jnp.concatenate([block] * FOLD, axis=0)
    left_ref[...] = jnp.where(row // TILE == (column // FOLD) % FOLD, block, 0.0).astype(
        jnp.bfloat16
    )


def factors(blocks, occupied_factor, virtual_factor):
    shape = jax.ShapeDtypeStruct((ROWS, ROWS), jnp.bfloat16)
    whole = pl.BlockSpec((ROWS, ROWS), lambda i, index: (0, 0))
    return pl.pallas_call(
        factor_kernel,
        out_shape=(shape, shape),
        grid_spec=pltpu.PrefetchScalarGridSpec(
            num_scalar_prefetch=1,
            grid=(1,),
            in_specs=[
                pl.BlockSpec((1, TILE, TILE), lambda i, index: (index[0], 0, 0)),
                pl.BlockSpec((1, TILE, TILE), lambda i, index: (index[1], 0, 0)),
            ],
            out_specs=(whole, whole),
        ),
        cost_estimate=pl.CostEstimate(
            flops=4_000_000, bytes_accessed=300_000, transcendentals=0
        ),
        name="factors",
    )(blocks, occupied_factor, virtual_factor)


def gram_kernel(parity_ref, left_ref, right_ref, tiles_ref, *refs):
    outs, half_ref, gram_ref = refs[:SPAN], refs[SPAN], refs[SPAN + 1]
    entries = tiles_ref.shape[1] * 2 // 5
    sources = ROWS // entries
    steps = ROWS // (FOLD * FOLD)
    for block in range(TILE * TILE // ROWS):
        span = pl.ds(block * sources, sources)
        first = tiles_ref[span, pl.ds(0, entries), :].reshape(ROWS, LANES)
        second = tiles_ref[span, pl.ds(entries, entries), :].reshape(ROWS, LANES)
        third = tiles_ref[span, pl.ds(2 * entries, entries // 2), :]
        third = jnp.concatenate([third[..., :TILE], third[..., TILE:]], axis=1)
        values = jnp.concatenate([first, second, third.reshape(ROWS, TILE)], axis=1)
        half = jnp.dot(right_ref[...], values, preferred_element_type=jnp.float32)
        half_ref[block] = half.astype(jnp.bfloat16).reshape(steps, FOLD * FOLD, SPAN * TILE)
    for step in range(steps):
        values = half_ref[:, step].reshape(ROWS, SPAN * TILE)
        panel = jnp.dot(left_ref[...], values, preferred_element_type=jnp.float32)
        panel = panel.astype(jnp.bfloat16)
        part = lax.dot_general(
            panel, panel, (((0,), (0,)), ((), ())), preferred_element_type=jnp.float32
        )
        if step == 0:
            gram_ref[...] = part
        else:
            gram_ref[...] += part
    odd = parity_ref[0] == 1
    scale = 0.5 / TILE
    for place in range(SPAN):
        swapped = place ^ 1 if place < SPAN - 1 else place
        rows = jnp.where(
            odd,
            gram_ref[pl.ds(swapped * TILE, TILE), :],
            gram_ref[pl.ds(place * TILE, TILE), :],
        )
        rows = rows * scale
        pieces = []
        for other in range(max(place - REACH, 0), min(place + REACH, SPAN - 1) + 1):
            turned = other ^ 1 if other < SPAN - 1 else other
            pieces.append(
                jnp.where(
                    odd,
                    rows[:, turned * TILE : (turned + 1) * TILE],
                    rows[:, other * TILE : (other + 1) * TILE],
                )
            )
        outs[place][...] = jnp.concatenate(pieces, axis=1)


def neighbours(place):
    return min(place + REACH, SPAN - 1) - max(place - REACH, 0) + 1


def gram(parity, left, right, tiles):
    vmem = pl.BlockSpec(memory_space=pltpu.VMEM)
    return pl.pallas_call(
        gram_kernel,
        out_shape=tuple(
            jax.ShapeDtypeStruct((TILE, TILE * neighbours(place)), jnp.float32)
            for place in range(SPAN)
        ),
        in_specs=[pl.BlockSpec(memory_space=pltpu.SMEM), vmem, vmem, vmem],
        out_specs=(vmem,) * SPAN,
        scratch_shapes=[
            pltpu.VMEM((TILE * TILE // ROWS, ROWS // (FOLD * FOLD), FOLD * FOLD, SPAN * TILE), jnp.bfloat16),
            pltpu.VMEM((SPAN * TILE, SPAN * TILE), jnp.float32),
        ],
        compiler_params=pltpu.CompilerParams(vmem_limit_bytes=32 * 1024 * 1024),
        name="gram",
    )(parity, left, right, tiles)


CHUNKS = 8
MAIN = 30
SPILL = 6
ROOM = MAIN + SPILL
UNIT = FOLD * FOLD
RECIPROCALS = (4096, 2048, 1366, 1024, 820)


def swap_halves(value):
    return jnp.concatenate([value[:, TILE:], value[:, :TILE]], axis=1)


def plan_tiles(list_ref, occupancy_ref, plan_ref, flag_ref):
    slots, count = list_ref.shape
    held, shed = SPAN * count, SPAN * count + count

    for index in range(SPAN * count):
        plan_ref[index] = 0
    for group in range(count):
        for j in range(slots):
            t = list_ref[j, group] - group
            t = jnp.where(t < 0, t + count, t)
            plan_ref[group * SPAN + t] = jnp.where(j < occupancy_ref[group], j + 1, -1)
    entries = [[plan_ref[group * SPAN + t] for t in range(SPAN)] for group in range(count)]

    def quotient(value, factor):
        return (value * factor) >> 12

    heres, factors = [], []
    for pair in range(count):
        here = jnp.int32(0)
        for t in range(SPAN):
            here += jnp.where(entries[(pair - t) % count][t] > 0, 1, 0)
        factor = jnp.int32(RECIPROCALS[-1])
        for d in range(SPAN - 1, 0, -1):
            factor = jnp.where(here <= d, RECIPROCALS[d - 1], factor)
        heres.append(here)
        factors.append(jnp.where(here > 0, factor, 0))
        plan_ref[held + pair] = here
    gives = [None] * count
    taken = jnp.int32(0)
    for _ in range(2):
        for pair in range(count - 1, -1, -1):
            here = heres[pair]
            excess = jnp.maximum(CHUNKS * here + taken - MAIN, 0)
            gives[pair] = jnp.minimum(quotient(excess + here - 1, factors[pair]), CHUNKS)
            taken = here * gives[pair]
    spills = jnp.bool_(False)
    for pair in range(count):
        after = (pair + 1) % count
        load = heres[pair] * (CHUNKS - gives[pair]) + heres[after] * gives[after]
        spills = spills | (load > MAIN)
        plan_ref[shed + pair] = gives[pair]
    flag_ref[0] = jnp.where(spills, 1, 0)

    @pl.when(spills)
    def _():
        for pair in range(count):
            listed = jnp.int32(0)
            before = jnp.int32(0)
            for t in range(SPAN):
                listed += jnp.where(entries[(pair - t) % count][t] != 0, 1, 0)
            for distance in range(1, SPAN):
                for t in range(distance):
                    before += jnp.where(entries[(pair - distance) % count][t] != 0, 1, 0)
            factor = jnp.int32(RECIPROCALS[-1])
            for d in range(SPAN - 1, 0, -1):
                factor = jnp.where(listed <= d, RECIPROCALS[d - 1], factor)
            give = quotient(CHUNKS * (2 * SPAN - before), factor)
            plan_ref[shed + pair] = jnp.where(listed > 0, give, 0)

    return entries, heres


def source_kernel(
    list_hbm, occupancy_hbm, blocks_hbm, tiles_hbm, virtual_hbm,
    main_hbm, spill_hbm, plan_ref, flag_ref,
    list_ref, occupancy_ref, blocks_ref, tiles_ref, virtual_ref, packed_ref,
    small_sem, virtual_sem, in_sem, main_sem, spill_sem,
):
    count = list_ref.shape[1]
    shed = SPAN * count + count
    parts = count // 4
    width = 4 * TILE
    small = [
        pltpu.make_async_copy(there, here, small_sem.at[index])
        for index, (there, here) in enumerate(
            ((blocks_hbm, blocks_ref), (list_hbm, list_ref), (occupancy_hbm, occupancy_ref))
        )
    ]
    for copy in small:
        copy.start()
    fetches = []
    for part in range(parts):
        lanes = pl.ds(part * width, width)
        fetches.append(
            pltpu.make_async_copy(
                tiles_hbm.at[:, :, lanes], tiles_ref.at[:, :, lanes], in_sem.at[part]
            )
        )
    small[0].wait()
    picks = []
    for pair in range(count):
        picks.append(
            pltpu.make_async_copy(
                virtual_hbm.at[blocks_ref[1, pair]], virtual_ref.at[pair], virtual_sem.at[pair]
            )
        )
        picks[-1].start()
    for copy in fetches:
        copy.start()
    small[1].wait()
    small[2].wait()
    entries, heres = plan_tiles(list_ref, occupancy_ref, plan_ref, flag_ref)
    gives = [plan_ref[shed + pair] for pair in range(count)]
    for copy in picks:
        copy.wait()

    low = lax.broadcasted_iota(jnp.int32, (1, LANES), 1) < TILE
    spread = (
        lax.broadcasted_iota(jnp.int32, (ROWS, TILE), 0) // FOLD
        == lax.broadcasted_iota(jnp.int32, (ROWS, TILE), 1)
    ).astype(jnp.bfloat16)
    diagonal = (
        lax.broadcasted_iota(jnp.int32, (ROWS, ROWS), 0) % FOLD
        == lax.broadcasted_iota(jnp.int32, (ROWS, ROWS), 1) // TILE
    ).astype(jnp.bfloat16)

    def send(dest):
        first = dest * (ROOM + 1)
        return (
            pltpu.make_async_copy(
                packed_ref.at[pl.ds(first, MAIN)], main_hbm.at[dest], main_sem.at[dest]
            ),
            pltpu.make_async_copy(
                packed_ref.at[pl.ds(first + MAIN, SPILL)], spill_hbm.at[dest], spill_sem.at[dest]
            ),
        )

    arrived = set()
    rights = {}
    written = set()
    sent = []
    for pair in [(index + 4) % count for index in range(count)]:
        previous = (pair - 1) % count
        for t in range(SPAN):
            part = ((pair - t) % count) // 4
            if part not in arrived:
                arrived.add(part)
                fetches[part].wait()
        if pair not in rights:
            couple = pair // 2 * 2
            block = lax.dot_general(
                spread,
                virtual_ref[couple : couple + 2].reshape(2 * TILE, TILE),
                (((1,), (1,)), ((), ())),
                preferred_element_type=jnp.float32,
            ).astype(jnp.bfloat16)
            turned = swap_halves(block)
            for side in range(2):
                double = jnp.where(low, turned, block) if side else jnp.where(low, block, turned)
                rights[couple + side] = jnp.concatenate([double, double], axis=1) * diagonal
        values, ranks = [], []
        rank = jnp.int32(0)
        for place in range(SPAN):
            t = SPAN - 1 - place
            group = (pair - t) % count
            entry = entries[group][t]
            columns = pl.ds((group // 2) * LANES, LANES)
            values.append(tiles_ref[jnp.maximum(entry - 1, 0), :, columns])
            ranks.append((entry > 0, rank))
            rank += jnp.where(entry > 0, 1, 0)
        parity = pair % 2
        lows = [values[place] for place in range(parity, SPAN, 2)]
        highs = [values[place] for place in range(1 - parity, SPAN, 2)]
        if parity == 0:
            highs.append(lows[-1])
        else:
            lows.append(highs[-1])
        joined = [jnp.where(low, a, b) for a, b in zip(lows, highs)]
        half = jnp.dot(
            rights[pair], jnp.concatenate(joined, axis=1), preferred_element_type=jnp.float32
        ).astype(jnp.bfloat16)
        here, give = heres[pair], gives[pair]
        base = previous * (ROOM + 1) + heres[previous] * (CHUNKS - gives[previous])
        starts = []
        for chunk in range(CHUNKS):
            starts.append(
                jnp.where(
                    chunk >= give,
                    pair * (ROOM + 1) + (chunk - give) * here,
                    base + chunk * here,
                )
            )
        middle = ROWS // 2
        for place in range(SPAN):
            piece = half[:, (place // 2) * LANES : (place // 2 + 1) * LANES]
            if (place + parity) % 2 == 0:
                folded = jnp.where(low, piece[:middle], swap_halves(piece[middle:]))
            else:
                folded = jnp.where(low, swap_halves(piece[:middle]), piece[middle:])
            found, rank = ranks[place]
            for chunk in range(CHUNKS):
                slot = jnp.where(found, starts[chunk] + rank, count * (ROOM + 1))
                packed_ref[slot] = folded[chunk * UNIT : (chunk + 1) * UNIT]
        written.add(pair)
        for dest in (pair, previous):
            if dest in written and (dest + 1) % count in written and dest not in sent:
                sent.append(dest)
                for copy in send(dest):
                    copy.start()
    for dest in sent:
        for copy in send(dest):
            copy.wait()


def source(three_index, virtual_factor, pair_list, occupancy, pair_blocks):
    count = pair_list.shape[0]
    smem = pl.BlockSpec(memory_space=pltpu.SMEM)
    hbm = pl.BlockSpec(memory_space=pltpu.HBM)
    return pl.pallas_call(
        source_kernel,
        out_shape=(
            jax.ShapeDtypeStruct((count, MAIN, UNIT, LANES), jnp.bfloat16),
            jax.ShapeDtypeStruct((count, SPILL, UNIT, LANES), jnp.bfloat16),
            jax.ShapeDtypeStruct(((SPAN + 2) * count,), jnp.int32),
            jax.ShapeDtypeStruct((1,), jnp.int32),
        ),
        in_specs=[hbm] * 5,
        out_specs=(hbm, hbm, smem, smem),
        scratch_shapes=[
            pltpu.SMEM(pair_list.shape[::-1], jnp.int32),
            pltpu.SMEM(occupancy.shape, jnp.int32),
            pltpu.SMEM(pair_blocks.shape[::-1], jnp.int32),
            pltpu.VMEM(three_index.shape, jnp.bfloat16),
            pltpu.VMEM((count,) + virtual_factor.shape[1:], jnp.bfloat16),
            pltpu.VMEM((count * (ROOM + 1) + 1, UNIT, LANES), jnp.bfloat16),
            pltpu.SemaphoreType.DMA((3,)),
            pltpu.SemaphoreType.DMA((count,)),
            pltpu.SemaphoreType.DMA((count // 4,)),
            pltpu.SemaphoreType.DMA((count,)),
            pltpu.SemaphoreType.DMA((count,)),
        ],
        compiler_params=pltpu.CompilerParams(vmem_limit_bytes=60 * 1024 * 1024),
        name="source",
    )(pair_list.T, occupancy, pair_blocks.T, three_index, virtual_factor)


def left_kernel(index_ref, first_ref, second_ref, left_ref):
    row = lax.broadcasted_iota(jnp.int32, (ROWS, ROWS), 0)
    column = lax.broadcasted_iota(jnp.int32, (ROWS, ROWS), 1)
    entry = lax.broadcasted_iota(jnp.int32, (TILE, ROWS), 1)
    spread = (
        (entry // UNIT) * FOLD + entry % FOLD
        == lax.broadcasted_iota(jnp.int32, (TILE, ROWS), 0)
    ).astype(jnp.bfloat16)
    for segment, occupied_ref in enumerate((first_ref, second_ref)):
        block = lax.dot_general(
            occupied_ref[0], spread, (((0,), (0,)), ((), ())), preferred_element_type=jnp.float32
        )
        block = jnp.concatenate([block] * FOLD, axis=0)
        left_ref[segment] = jnp.where(
            row // TILE == (column // FOLD) % FOLD, block, 0.0
        ).astype(jnp.bfloat16)


def left_factors(blocks, occupied_factor):
    return pl.pallas_call(
        left_kernel,
        out_shape=jax.ShapeDtypeStruct((2, ROWS, ROWS), jnp.bfloat16),
        grid_spec=pltpu.PrefetchScalarGridSpec(
            num_scalar_prefetch=1,
            grid=(1,),
            in_specs=[
                pl.BlockSpec((1, TILE, TILE), lambda i, index: (index[0], 0, 0)),
                pl.BlockSpec((1, TILE, TILE), lambda i, index: (index[1], 0, 0)),
            ],
            out_specs=pl.BlockSpec((2, ROWS, ROWS), lambda i, index: (0, 0, 0)),
        ),
        cost_estimate=pl.CostEstimate(
            flops=4_000_000, bytes_accessed=300_000, transcendentals=0
        ),
        name="left_factors",
    )(blocks, occupied_factor, occupied_factor)


WIDE = SPAN + 1


def shared_kernel(own_ref, plan_ref, left_ref, main_ref, spill_ref, *refs):
    outs, gram_ref = refs[:WIDE], refs[WIDE]
    count = main_ref.shape[0]
    held, shed = SPAN * count, SPAN * count + count
    own = own_ref[0]
    low = lax.broadcasted_iota(jnp.int32, (1, LANES), 1) < TILE
    gram_ref[...] = jnp.zeros_like(gram_ref)
    for segment in range(2):
        pair = own + segment
        pair = jnp.where(pair >= count, pair - count, pair)
        here, give = plan_ref[held + pair], plan_ref[shed + pair]
        if segment == 0:
            units, base = CHUNKS - give, jnp.int32(0)
            kept = units * here
        else:
            units, base = give, kept
        ranks = []
        rank = jnp.int32(0)
        for place in range(SPAN):
            t = SPAN - 1 - place
            group = pair - t
            group = jnp.where(group < 0, group + count, group)
            found = plan_ref[group * SPAN + t] > 0
            ranks.append((found, rank))
            rank += jnp.where(found, 1, 0)

        def unit(index, carry, segment=segment, here=here, base=base, ranks=ranks):
            values = []
            for found, rank in ranks:
                slot = base + index * here + rank
                value = jnp.where(
                    slot < MAIN,
                    main_ref[:, jnp.minimum(slot, MAIN - 1)],
                    spill_ref[:, jnp.clip(slot - MAIN, 0, SPILL - 1)],
                )
                value = jnp.where(found, value, jnp.zeros_like(value))
                values.append(value.reshape(ROWS, LANES))
            panel = jnp.dot(
                left_ref[segment],
                jnp.concatenate(values, axis=1),
                preferred_element_type=jnp.float32,
            ).astype(jnp.bfloat16)
            tops, bottoms = [], []
            for couple in range(WIDE // 2):
                lows, highs = [], []
                for side in range(2):
                    place = 2 * couple + side - segment
                    if 0 <= place < SPAN:
                        piece = panel[:, place * LANES : (place + 1) * LANES]
                    else:
                        piece = jnp.zeros((ROWS, LANES), jnp.bfloat16)
                    turned = swap_halves(piece)
                    lows.append(piece if side == 0 else turned)
                    highs.append(turned if side == 0 else piece)
                tops.append(jnp.where(low, lows[0], lows[1]))
                bottoms.append(jnp.where(low, highs[0], highs[1]))
            stack = jnp.concatenate(
                [jnp.concatenate(tops, axis=1), jnp.concatenate(bottoms, axis=1)], axis=0
            )
            gram_ref[...] += lax.dot_general(
                stack, stack, (((0,), (0,)), ((), ())), preferred_element_type=jnp.float32
            )
            return carry

        lax.fori_loop(0, units, unit, 0)
    for place in range(WIDE):
        first, last = max(place - REACH, 0), min(place + REACH, WIDE - 1)
        outs[place][...] = (
            gram_ref[pl.ds(place * TILE, TILE), :][:, first * TILE : (last + 1) * TILE]
            * (0.5 / TILE)
        )


def shared_gram(own, plan, left, main, spill):
    vmem = pl.BlockSpec(memory_space=pltpu.VMEM)
    smem = pl.BlockSpec(memory_space=pltpu.SMEM)
    widths = [
        TILE * (min(place + REACH, WIDE - 1) - max(place - REACH, 0) + 1) for place in range(WIDE)
    ]
    return pl.pallas_call(
        shared_kernel,
        out_shape=tuple(jax.ShapeDtypeStruct((TILE, width), jnp.float32) for width in widths),
        in_specs=[smem, smem, vmem, vmem, vmem],
        out_specs=(vmem,) * WIDE,
        scratch_shapes=[pltpu.VMEM((WIDE * TILE, WIDE * TILE), jnp.float32)],
        compiler_params=pltpu.CompilerParams(vmem_limit_bytes=32 * 1024 * 1024),
        name="shared_gram",
    )(own, plan, left, main, spill)


def assemble(parts, shifts, count):
    total = None
    for place, (part, shift) in enumerate(zip(parts, shifts)):
        if shift:
            part = lax.ppermute(
                part, "row", [(device, (device + shift) % count) for device in range(count)]
            )
        before = max(REACH - place, 0) * TILE
        after = (2 * REACH + 1) * TILE - before - part.shape[1]
        part = jnp.pad(part, ((0, 0), (before, after)))
        total = part if total is None else total + part
    return total


def exchange(value):
    return lax.all_to_all(value, "row", split_axis=0, concat_axis=0, tiled=True)


def local_balanced(
    three_index, occupied_factor, virtual_factor, pair_list, occupancy, pair_blocks
):
    count = lax.axis_size("row")
    own = lax.axis_index("row")
    main, spill, plan, flag = source(
        three_index, virtual_factor, pair_list, occupancy, pair_blocks
    )
    main = exchange(main)
    spill = lax.cond(flag[0] > 0, exchange, jnp.zeros_like, spill)
    pairs = jnp.stack([own, lax.rem(own + 1, count)])
    left = left_factors(jnp.take(pair_blocks[:, 0], pairs), occupied_factor)
    parts = shared_gram(own.reshape(1).astype(jnp.int32), plan, left, main, spill)
    return assemble(parts, range(1 - SPAN, 2), count)


def local_padded(three_index, occupied_factor, virtual_factor, pair_list, occupancy, pair_blocks):
    count = lax.axis_size("row")
    own = lax.axis_index("row")
    packed = pack(three_index, pair_list, occupancy)
    tiles = exchange(packed)
    blocks = lax.dynamic_index_in_dim(pair_blocks, own, 0, keepdims=False)
    left, right = factors(blocks, occupied_factor, virtual_factor)
    parity = lax.rem(own, 2).reshape(1).astype(jnp.int32)
    parts = gram(parity, left, right, tiles)
    return assemble(parts, range(1 - SPAN, 1), count)


def local(three_index, *rest):
    whole_rows = three_index.shape[1] == ROWS
    return (local_balanced if whole_rows else local_padded)(three_index, *rest)


def solution(mesh):
    placed = (
        P(None, "row", "grp"),
        P("grp", None, None),
        P("grp", None, None),
        P("grp", None),
        P("grp"),
        P(),
    )
    return jax.shard_map(
        local, mesh=mesh, in_specs=placed, out_specs=P(("grp", "row"), None), check_vma=False
    )
```

```python
import functools

import jax
import jax.numpy as jnp
from jax import lax
from jax.experimental import pallas as pl
from jax.experimental.pallas import tpu as pltpu
from jax.sharding import PartitionSpec as P

TILE = 64
SPAN = 5
REACH = 2
LANES = 128
ROWS = 256
FOLD = ROWS // TILE


def pack_kernel(list_ref, occupancy_ref, source_ref, packed_ref):
    count, slots = list_ref.shape
    entries = source_ref.shape[1]
    low_half = lax.broadcasted_iota(jnp.int32, (1, LANES), 1) < TILE

    def pick(group, pair):
        slot = jnp.int32(0)
        found = jnp.int32(0)
        for j in range(slots):
            hit = (list_ref[group, j] == pair) & (j < occupancy_ref[group])
            slot = jnp.where(hit, j, slot)
            found = jnp.where(hit, 1, found)
        return slot, found

    def columns(group):
        return pl.ds(pl.multiple_of((group // 2) * LANES, LANES), LANES)

    def step(index, carry):
        for parity in range(2):
            pair = 2 * index + parity
            for couple in range(2):
                first = lax.rem(pair - 4 + 2 * couple + count, count)
                second = lax.rem(pair - 3 + 2 * couple + count, count)
                low, high = (first, second) if parity == 0 else (second, first)
                low_slot, low_found = pick(low, pair)
                high_slot, high_found = pick(high, pair)
                found = jnp.where(low_half, low_found, high_found) > 0
                value = jnp.where(
                    low_half,
                    source_ref[low_slot, :, columns(low)],
                    source_ref[high_slot, :, columns(high)],
                )
                packed_ref[pair, pl.ds(couple * entries, entries), :] = jnp.where(
                    found, value, jnp.zeros_like(value)
                )
            slot, found = pick(pair, pair)
            value = source_ref[slot, :, columns(pair)]
            value = jnp.where(found > 0, value, jnp.zeros_like(value))
            upper, under = value[: entries // 2], value[entries // 2 :]
            if parity == 0:
                folded = jnp.concatenate([upper[:, :TILE], under[:, :TILE]], axis=1)
            else:
                folded = jnp.concatenate([upper[:, TILE:], under[:, TILE:]], axis=1)
            packed_ref[pair, pl.ds(2 * entries, entries // 2), :] = folded
        return carry

    lax.fori_loop(0, count // 2, step, 0)


def pack(three_index, pair_list, occupancy):
    count = pair_list.shape[0]
    entries = three_index.shape[1]
    return pl.pallas_call(
        pack_kernel,
        out_shape=jax.ShapeDtypeStruct((count, 5 * entries // 2, LANES), jnp.bfloat16),
        in_specs=[
            pl.BlockSpec(memory_space=pltpu.SMEM),
            pl.BlockSpec(memory_space=pltpu.SMEM),
            pl.BlockSpec(memory_space=pltpu.VMEM),
        ],
        out_specs=pl.BlockSpec(memory_space=pltpu.VMEM),
        compiler_params=pltpu.CompilerParams(vmem_limit_bytes=32 * 1024 * 1024),
        name="pack",
    )(pair_list, occupancy, three_index)


def factor_kernel(index_ref, occupied_ref, virtual_ref, left_ref, right_ref):
    row = lax.broadcasted_iota(jnp.int32, (ROWS, ROWS), 0)
    column = lax.broadcasted_iota(jnp.int32, (ROWS, ROWS), 1)
    spread = (
        lax.broadcasted_iota(jnp.int32, (ROWS, TILE), 0) // FOLD
        == lax.broadcasted_iota(jnp.int32, (ROWS, TILE), 1)
    ).astype(jnp.bfloat16)
    block = lax.dot_general(
        spread, virtual_ref[0], (((1,), (1,)), ((), ())), preferred_element_type=jnp.float32
    )
    block = jnp.concatenate([block] * FOLD, axis=1)
    right_ref[...] = jnp.where(row % FOLD == column // TILE, block, 0.0).astype(jnp.bfloat16)
    entry = lax.broadcasted_iota(jnp.int32, (TILE, ROWS), 1)
    spread = (
        (entry // (FOLD * FOLD)) * FOLD + entry % FOLD
        == lax.broadcasted_iota(jnp.int32, (TILE, ROWS), 0)
    ).astype(jnp.bfloat16)
    block = lax.dot_general(
        occupied_ref[0], spread, (((0,), (0,)), ((), ())), preferred_element_type=jnp.float32
    )
    block = jnp.concatenate([block] * FOLD, axis=0)
    left_ref[...] = jnp.where(row // TILE == (column // FOLD) % FOLD, block, 0.0).astype(
        jnp.bfloat16
    )


def factors(blocks, occupied_factor, virtual_factor):
    shape = jax.ShapeDtypeStruct((ROWS, ROWS), jnp.bfloat16)
    whole = pl.BlockSpec((ROWS, ROWS), lambda i, index: (0, 0))
    return pl.pallas_call(
        factor_kernel,
        out_shape=(shape, shape),
        grid_spec=pltpu.PrefetchScalarGridSpec(
            num_scalar_prefetch=1,
            grid=(1,),
            in_specs=[
                pl.BlockSpec((1, TILE, TILE), lambda i, index: (index[0], 0, 0)),
                pl.BlockSpec((1, TILE, TILE), lambda i, index: (index[1], 0, 0)),
            ],
            out_specs=(whole, whole),
        ),
        cost_estimate=pl.CostEstimate(
            flops=4_000_000, bytes_accessed=300_000, transcendentals=0
        ),
        name="factors",
    )(blocks, occupied_factor, virtual_factor)


def gram_kernel(parity_ref, left_ref, right_ref, tiles_ref, *refs):
    outs, half_ref, gram_ref = refs[:SPAN], refs[SPAN], refs[SPAN + 1]
    entries = tiles_ref.shape[1] * 2 // 5
    sources = ROWS // entries
    steps = ROWS // (FOLD * FOLD)
    for block in range(TILE * TILE // ROWS):
        span = pl.ds(block * sources, sources)
        first = tiles_ref[span, pl.ds(0, entries), :].reshape(ROWS, LANES)
        second = tiles_ref[span, pl.ds(entries, entries), :].reshape(ROWS, LANES)
        third = tiles_ref[span, pl.ds(2 * entries, entries // 2), :]
        third = jnp.concatenate([third[..., :TILE], third[..., TILE:]], axis=1)
        values = jnp.concatenate([first, second, third.reshape(ROWS, TILE)], axis=1)
        half = jnp.dot(right_ref[...], values, preferred_element_type=jnp.float32)
        half_ref[block] = half.astype(jnp.bfloat16).reshape(steps, FOLD * FOLD, SPAN * TILE)
    for step in range(steps):
        values = half_ref[:, step].reshape(ROWS, SPAN * TILE)
        panel = jnp.dot(left_ref[...], values, preferred_element_type=jnp.float32)
        panel = panel.astype(jnp.bfloat16)
        part = lax.dot_general(
            panel, panel, (((0,), (0,)), ((), ())), preferred_element_type=jnp.float32
        )
        if step == 0:
            gram_ref[...] = part
        else:
            gram_ref[...] += part
    odd = parity_ref[0] == 1
    scale = 0.5 / TILE
    for place in range(SPAN):
        swapped = place ^ 1 if place < SPAN - 1 else place
        rows = jnp.where(
            odd,
            gram_ref[pl.ds(swapped * TILE, TILE), :],
            gram_ref[pl.ds(place * TILE, TILE), :],
        )
        rows = rows * scale
        pieces = []
        for other in range(max(place - REACH, 0), min(place + REACH, SPAN - 1) + 1):
            turned = other ^ 1 if other < SPAN - 1 else other
            pieces.append(
                jnp.where(
                    odd,
                    rows[:, turned * TILE : (turned + 1) * TILE],
                    rows[:, other * TILE : (other + 1) * TILE],
                )
            )
        outs[place][...] = jnp.concatenate(pieces, axis=1)


def neighbours(place):
    return min(place + REACH, SPAN - 1) - max(place - REACH, 0) + 1


def gram(parity, left, right, tiles):
    vmem = pl.BlockSpec(memory_space=pltpu.VMEM)
    return pl.pallas_call(
        gram_kernel,
        out_shape=tuple(
            jax.ShapeDtypeStruct((TILE, TILE * neighbours(place)), jnp.float32)
            for place in range(SPAN)
        ),
        in_specs=[pl.BlockSpec(memory_space=pltpu.SMEM), vmem, vmem, vmem],
        out_specs=(vmem,) * SPAN,
        scratch_shapes=[
            pltpu.VMEM((TILE * TILE // ROWS, ROWS // (FOLD * FOLD), FOLD * FOLD, SPAN * TILE), jnp.bfloat16),
            pltpu.VMEM((SPAN * TILE, SPAN * TILE), jnp.float32),
        ],
        compiler_params=pltpu.CompilerParams(vmem_limit_bytes=32 * 1024 * 1024),
        name="gram",
    )(parity, left, right, tiles)


CHUNKS = 8
MAIN = 30
SPILL = 6
ROOM = MAIN + SPILL
UNIT = FOLD * FOLD
RECIPROCALS = (4096, 2048, 1366, 1024, 820)


def swap_halves(value):
    return jnp.concatenate([value[:, TILE:], value[:, :TILE]], axis=1)


def plan_tiles(list_ref, occupancy_ref, plan_ref, flag_ref):
    slots, count = list_ref.shape
    held, shed = SPAN * count, SPAN * count + count

    for index in range(SPAN * count):
        plan_ref[index] = 0
    for group in range(count):
        for j in range(slots):
            t = list_ref[j, group] - group
            t = jnp.where(t < 0, t + count, t)
            plan_ref[group * SPAN + t] = jnp.where(j < occupancy_ref[group], j + 1, -1)
    entries = [[plan_ref[group * SPAN + t] for t in range(SPAN)] for group in range(count)]

    def quotient(value, factor):
        return (value * factor) >> 12

    heres, factors = [], []
    for pair in range(count):
        here = jnp.int32(0)
        for t in range(SPAN):
            here += jnp.where(entries[(pair - t) % count][t] > 0, 1, 0)
        factor = jnp.int32(RECIPROCALS[-1])
        for d in range(SPAN - 1, 0, -1):
            factor = jnp.where(here <= d, RECIPROCALS[d - 1], factor)
        heres.append(here)
        factors.append(jnp.where(here > 0, factor, 0))
        plan_ref[held + pair] = here
    gives = [None] * count
    taken = jnp.int32(0)
    for _ in range(2):
        for pair in range(count - 1, -1, -1):
            here = heres[pair]
            excess = jnp.maximum(CHUNKS * here + taken - MAIN, 0)
            gives[pair] = jnp.minimum(quotient(excess + here - 1, factors[pair]), CHUNKS)
            taken = here * gives[pair]
    spills = jnp.bool_(False)
    for pair in range(count):
        after = (pair + 1) % count
        load = heres[pair] * (CHUNKS - gives[pair]) + heres[after] * gives[after]
        spills = spills | (load > MAIN)
        plan_ref[shed + pair] = gives[pair]
    flag_ref[0] = jnp.where(spills, 1, 0)

    @pl.when(spills)
    def _():
        for pair in range(count):
            listed = jnp.int32(0)
            before = jnp.int32(0)
            for t in range(SPAN):
                listed += jnp.where(entries[(pair - t) % count][t] != 0, 1, 0)
            for distance in range(1, SPAN):
                for t in range(distance):
                    before += jnp.where(entries[(pair - distance) % count][t] != 0, 1, 0)
            factor = jnp.int32(RECIPROCALS[-1])
            for d in range(SPAN - 1, 0, -1):
                factor = jnp.where(listed <= d, RECIPROCALS[d - 1], factor)
            give = quotient(CHUNKS * (2 * SPAN - before), factor)
            plan_ref[shed + pair] = jnp.where(listed > 0, give, 0)

    return entries, heres


def source_kernel(
    list_hbm, occupancy_hbm, blocks_hbm, tiles_hbm, virtual_hbm,
    main_hbm, spill_hbm, plan_ref, flag_ref,
    list_ref, occupancy_ref, blocks_ref, tiles_ref, virtual_ref, packed_ref,
    small_sem, virtual_sem, in_sem, main_sem, spill_sem,
):
    count = list_ref.shape[1]
    shed = SPAN * count + count
    parts = count // 4
    width = 4 * TILE
    small = [
        pltpu.make_async_copy(there, here, small_sem.at[index])
        for index, (there, here) in enumerate(
            ((blocks_hbm, blocks_ref), (list_hbm, list_ref), (occupancy_hbm, occupancy_ref))
        )
    ]
    for copy in small:
        copy.start()
    fetches = []
    for part in range(parts):
        lanes = pl.ds(part * width, width)
        fetches.append(
            pltpu.make_async_copy(
                tiles_hbm.at[:, :, lanes], tiles_ref.at[:, :, lanes], in_sem.at[part]
            )
        )
    for copy in fetches:
        copy.start()
    small[0].wait()
    picks = []
    for pair in range(count):
        picks.append(
            pltpu.make_async_copy(
                virtual_hbm.at[blocks_ref[1, pair]], virtual_ref.at[pair], virtual_sem.at[pair]
            )
        )
        picks[-1].start()
    small[1].wait()
    small[2].wait()
    entries, heres = plan_tiles(list_ref, occupancy_ref, plan_ref, flag_ref)
    gives = [plan_ref[shed + pair] for pair in range(count)]
    for copy in picks:
        copy.wait()

    low = lax.broadcasted_iota(jnp.int32, (1, LANES), 1) < TILE
    spread = (
        lax.broadcasted_iota(jnp.int32, (ROWS, TILE), 0) // FOLD
        == lax.broadcasted_iota(jnp.int32, (ROWS, TILE), 1)
    ).astype(jnp.bfloat16)
    diagonal = (
        lax.broadcasted_iota(jnp.int32, (ROWS, ROWS), 0) % FOLD
        == lax.broadcasted_iota(jnp.int32, (ROWS, ROWS), 1) // TILE
    ).astype(jnp.bfloat16)

    def send(dest):
        first = dest * (ROOM + 1)
        return pltpu.make_async_copy(
            packed_ref.at[pl.ds(first, MAIN)], main_hbm.at[dest], main_sem.at[dest]
        )

    def send_spill(dest):
        first = dest * (ROOM + 1) + MAIN
        return pltpu.make_async_copy(
            packed_ref.at[pl.ds(first, SPILL)], spill_hbm.at[dest], spill_sem.at[dest]
        )

    arrived = set()
    rights = {}
    written = set()
    sent = []
    for pair in [(index + 4) % count for index in range(count)]:
        previous = (pair - 1) % count
        for t in range(SPAN):
            part = ((pair - t) % count) // 4
            if part not in arrived:
                arrived.add(part)
                fetches[part].wait()
        if pair not in rights:
            couple = pair // 2 * 2
            block = lax.dot_general(
                spread,
                virtual_ref[couple : couple + 2].reshape(2 * TILE, TILE),
                (((1,), (1,)), ((), ())),
                preferred_element_type=jnp.float32,
            ).astype(jnp.bfloat16)
            turned = swap_halves(block)
            for side in range(2):
                double = jnp.where(low, turned, block) if side else jnp.where(low, block, turned)
                rights[couple + side] = jnp.concatenate([double, double], axis=1) * diagonal
        values, ranks = [], []
        rank = jnp.int32(0)
        for place in range(SPAN):
            t = SPAN - 1 - place
            group = (pair - t) % count
            entry = entries[group][t]
            columns = pl.ds((group // 2) * LANES, LANES)
            values.append(tiles_ref[jnp.maximum(entry - 1, 0), :, columns])
            ranks.append((entry > 0, rank))
            rank += jnp.where(entry > 0, 1, 0)
        parity = pair % 2
        lows = [values[place] for place in range(parity, SPAN, 2)]
        highs = [values[place] for place in range(1 - parity, SPAN, 2)]
        if parity == 0:
            highs.append(lows[-1])
        else:
            lows.append(highs[-1])
        joined = [jnp.where(low, a, b) for a, b in zip(lows, highs)]
        half = jnp.dot(
            rights[pair], jnp.concatenate(joined, axis=1), preferred_element_type=jnp.float32
        ).astype(jnp.bfloat16)
        here, give = heres[pair], gives[pair]
        base = previous * (ROOM + 1) + heres[previous] * (CHUNKS - gives[previous])
        starts = []
        for chunk in range(CHUNKS):
            starts.append(
                jnp.where(
                    chunk >= give,
                    pair * (ROOM + 1) + (chunk - give) * here,
                    base + chunk * here,
                )
            )
        middle = ROWS // 2
        for place in range(SPAN):
            piece = half[:, (place // 2) * LANES : (place // 2 + 1) * LANES]
            if (place + parity) % 2 == 0:
                folded = jnp.where(low, piece[:middle], swap_halves(piece[middle:]))
            else:
                folded = jnp.where(low, swap_halves(piece[:middle]), piece[middle:])
            found, rank = ranks[place]
            for chunk in range(CHUNKS):
                slot = jnp.where(found, starts[chunk] + rank, count * (ROOM + 1))
                packed_ref[slot] = folded[chunk * UNIT : (chunk + 1) * UNIT]
        written.add(pair)
        for dest in (pair, previous):
            if dest in written and (dest + 1) % count in written and dest not in sent:
                sent.append(dest)
                send(dest).start()

    @pl.when(flag_ref[0] > 0)
    def _():
        for dest in range(count):
            send_spill(dest).start()
        for dest in range(count):
            send_spill(dest).wait()

    for dest in sent:
        send(dest).wait()


def source(three_index, virtual_factor, pair_list, occupancy, pair_blocks):
    count = pair_list.shape[0]
    smem = pl.BlockSpec(memory_space=pltpu.SMEM)
    hbm = pl.BlockSpec(memory_space=pltpu.HBM)
    return pl.pallas_call(
        source_kernel,
        out_shape=(
            jax.ShapeDtypeStruct((count, MAIN, UNIT, LANES), jnp.bfloat16),
            jax.ShapeDtypeStruct((count, SPILL, UNIT, LANES), jnp.bfloat16),
            jax.ShapeDtypeStruct(((SPAN + 2) * count,), jnp.int32),
            jax.ShapeDtypeStruct((1,), jnp.int32),
        ),
        in_specs=[hbm] * 5,
        out_specs=(hbm, hbm, smem, smem),
        scratch_shapes=[
            pltpu.SMEM(pair_list.shape[::-1], jnp.int32),
            pltpu.SMEM(occupancy.shape, jnp.int32),
            pltpu.SMEM(pair_blocks.shape[::-1], jnp.int32),
            pltpu.VMEM(three_index.shape, jnp.bfloat16),
            pltpu.VMEM((count,) + virtual_factor.shape[1:], jnp.bfloat16),
            pltpu.VMEM((count * (ROOM + 1) + 1, UNIT, LANES), jnp.bfloat16),
            pltpu.SemaphoreType.DMA((3,)),
            pltpu.SemaphoreType.DMA((count,)),
            pltpu.SemaphoreType.DMA((count // 4,)),
            pltpu.SemaphoreType.DMA((count,)),
            pltpu.SemaphoreType.DMA((count,)),
        ],
        compiler_params=pltpu.CompilerParams(vmem_limit_bytes=60 * 1024 * 1024),
        name="source",
    )(pair_list.T, occupancy, pair_blocks.T, three_index, virtual_factor)


def left_kernel(own_ref, blocks_hbm, occupied_hbm, left_ref, blocks_ref, occupied_ref, sem):
    count = blocks_ref.shape[1]
    fetch = pltpu.make_async_copy(blocks_hbm, blocks_ref, sem.at[0])
    fetch.start()
    fetch.wait()
    copies = []
    for segment in range(2):
        pair = own_ref[0] + segment
        pair = jnp.where(pair >= count, pair - count, pair)
        copies.append(
            pltpu.make_async_copy(
                occupied_hbm.at[blocks_ref[0, pair]], occupied_ref.at[segment], sem.at[segment + 1]
            )
        )
        copies[-1].start()
    row = lax.broadcasted_iota(jnp.int32, (ROWS, ROWS), 0)
    column = lax.broadcasted_iota(jnp.int32, (ROWS, ROWS), 1)
    entry = lax.broadcasted_iota(jnp.int32, (TILE, ROWS), 1)
    spread = (
        (entry // UNIT) * FOLD + entry % FOLD
        == lax.broadcasted_iota(jnp.int32, (TILE, ROWS), 0)
    ).astype(jnp.bfloat16)
    for segment in range(2):
        copies[segment].wait()
        block = lax.dot_general(
            occupied_ref[segment],
            spread,
            (((0,), (0,)), ((), ())),
            preferred_element_type=jnp.float32,
        )
        block = jnp.concatenate([block] * FOLD, axis=0)
        left_ref[segment] = jnp.where(
            row // TILE == (column // FOLD) % FOLD, block, 0.0
        ).astype(jnp.bfloat16)


def left_factors(own, pair_blocks, occupied_factor):
    hbm = pl.BlockSpec(memory_space=pltpu.HBM)
    return pl.pallas_call(
        left_kernel,
        out_shape=jax.ShapeDtypeStruct((2, ROWS, ROWS), jnp.bfloat16),
        in_specs=[pl.BlockSpec(memory_space=pltpu.SMEM), hbm, hbm],
        out_specs=pl.BlockSpec(memory_space=pltpu.VMEM),
        scratch_shapes=[
            pltpu.SMEM(pair_blocks.shape[::-1], jnp.int32),
            pltpu.VMEM((2,) + occupied_factor.shape[1:], jnp.bfloat16),
            pltpu.SemaphoreType.DMA((3,)),
        ],
        cost_estimate=pl.CostEstimate(
            flops=4_000_000, bytes_accessed=300_000, transcendentals=0
        ),
        compiler_params=pltpu.CompilerParams(vmem_limit_bytes=16 * 1024 * 1024),
        name="left_factors",
    )(own, pair_blocks.T, occupied_factor)


WIDE = SPAN + 1
UNROLL = 2


def shared_kernel(spilled, own_ref, plan_ref, left_ref, main_ref, *refs):
    spill_ref, refs = (refs[0], refs[1:]) if spilled else (None, refs)
    outs, first_ref, rest_ref = refs[:WIDE], refs[WIDE], refs[WIDE + 1]
    count = main_ref.shape[0]
    held, shed = SPAN * count, SPAN * count + count
    own = own_ref[0]
    after = jnp.where(own == count - 1, 0, own + 1)
    rows_with_rows = (((1,), (1,)), ((), ()))
    first_ref[...] = jnp.zeros_like(first_ref)
    rest_ref[...] = jnp.zeros_like(rest_ref)

    def tiles_of(pair, shift):
        found, ranks = [False] * WIDE, [0] * WIDE
        rank = jnp.int32(0)
        for place in range(SPAN):
            t = SPAN - 1 - place
            group = pair - t
            group = jnp.where(group < 0, group + count, group)
            found[place + shift] = plan_ref[group * SPAN + t] > 0
            ranks[place + shift] = rank
            rank += jnp.where(found[place + shift], 1, 0)
        return found, ranks

    own_here, after_here = plan_ref[held + own], plan_ref[held + after]
    own_units = CHUNKS - plan_ref[shed + own]
    units = own_units + plan_ref[shed + after]
    own_found, own_ranks = tiles_of(own, 0)
    after_found, after_ranks = tiles_of(after, 1)

    def gather(index):
        second = index >= own_units
        here = jnp.where(second, after_here, own_here)
        base = jnp.where(second, own_units * own_here, 0)
        base += jnp.where(second, index - own_units, index) * here
        values = []
        for place in range(WIDE):
            found = jnp.where(second, after_found[place], own_found[place])
            found = found & (index < units)
            slot = base + jnp.where(second, after_ranks[place], own_ranks[place])
            slot = jnp.where(found, slot, 0)
            value = main_ref[:, jnp.minimum(slot, MAIN - 1)]
            if spilled:
                value = jnp.where(
                    slot < MAIN, value, spill_ref[:, jnp.clip(slot - MAIN, 0, SPILL - 1)]
                )
            value = jnp.where(found, value, jnp.zeros_like(value))
            values.append(value.reshape(ROWS, LANES))
        return lax.dot_general(
            jnp.concatenate(values, axis=1).T,
            left_ref[jnp.where(second, 1, 0)],
            rows_with_rows,
            preferred_element_type=jnp.float32,
        ).astype(jnp.bfloat16)

    def step(index, carry):
        for inner in range(UNROLL):
            panel = gather(UNROLL * index + inner).reshape(WIDE, 2, TILE, ROWS)
            stack = jnp.concatenate(
                [panel[:, half].reshape(WIDE * TILE, ROWS) for half in range(2)], axis=1
            )
            first = stack[:LANES]
            first_ref[...] += lax.dot_general(
                first, first, rows_with_rows, preferred_element_type=jnp.float32
            )
            rest_ref[...] += lax.dot_general(
                stack, stack[LANES:], rows_with_rows, preferred_element_type=jnp.float32
            )
        return carry

    lax.fori_loop(0, (units + UNROLL - 1) // UNROLL, step, 0)

    turned = rest_ref[pl.ds(0, LANES), :][:, :LANES].T
    scale = 0.5 / TILE
    for place in range(WIDE):
        rows = rest_ref[pl.ds(place * TILE, TILE), :]
        if place < 2:
            left = first_ref[pl.ds(place * TILE, TILE), :]
        else:
            left = turned[(place - 2) * TILE : (place - 1) * TILE] if place < 4 else rows[:, :LANES]
        rows = jnp.concatenate([left, rows], axis=1)
        first, last = max(place - REACH, 0), min(place + REACH, WIDE - 1)
        outs[place][...] = rows[:, first * TILE : (last + 1) * TILE] * scale


def shared_gram(own, plan, left, *tiles):
    vmem = pl.BlockSpec(memory_space=pltpu.VMEM)
    smem = pl.BlockSpec(memory_space=pltpu.SMEM)
    widths = [
        TILE * (min(place + REACH, WIDE - 1) - max(place - REACH, 0) + 1) for place in range(WIDE)
    ]
    return pl.pallas_call(
        functools.partial(shared_kernel, len(tiles) > 1),
        out_shape=tuple(jax.ShapeDtypeStruct((TILE, width), jnp.float32) for width in widths),
        in_specs=[smem, smem, vmem] + [vmem] * len(tiles),
        out_specs=(vmem,) * WIDE,
        scratch_shapes=[
            pltpu.VMEM((LANES, LANES), jnp.float32),
            pltpu.VMEM((WIDE * TILE, WIDE * TILE - LANES), jnp.float32),
        ],
        compiler_params=pltpu.CompilerParams(vmem_limit_bytes=32 * 1024 * 1024),
        name="shared_gram",
    )(own, plan, left, *tiles)


def assemble(parts, shifts, count):
    total = None
    for place, (part, shift) in enumerate(zip(parts, shifts)):
        if shift:
            part = lax.ppermute(
                part, "row", [(device, (device + shift) % count) for device in range(count)]
            )
        before = max(REACH - place, 0) * TILE
        after = (2 * REACH + 1) * TILE - before - part.shape[1]
        part = jnp.pad(part, ((0, 0), (before, after)))
        total = part if total is None else total + part
    return total


def exchange(value):
    return lax.all_to_all(value, "row", split_axis=0, concat_axis=0, tiled=True)


def local_balanced(
    three_index, occupied_factor, virtual_factor, pair_list, occupancy, pair_blocks
):
    count = lax.axis_size("row")
    own = lax.axis_index("row")
    main, spill, plan, flag = source(
        three_index, virtual_factor, pair_list, occupancy, pair_blocks
    )
    main = exchange(main)
    own = own.reshape(1).astype(jnp.int32)
    left = left_factors(own, pair_blocks, occupied_factor)
    parts = lax.cond(
        flag[0] > 0,
        lambda spill: shared_gram(own, plan, left, main, exchange(spill)),
        lambda spill: shared_gram(own, plan, left, main),
        spill,
    )
    return assemble(parts, range(1 - SPAN, 2), count)


def local_padded(three_index, occupied_factor, virtual_factor, pair_list, occupancy, pair_blocks):
    count = lax.axis_size("row")
    own = lax.axis_index("row")
    packed = pack(three_index, pair_list, occupancy)
    tiles = exchange(packed)
    blocks = lax.dynamic_index_in_dim(pair_blocks, own, 0, keepdims=False)
    left, right = factors(blocks, occupied_factor, virtual_factor)
    parity = lax.rem(own, 2).reshape(1).astype(jnp.int32)
    parts = gram(parity, left, right, tiles)
    return assemble(parts, range(1 - SPAN, 1), count)


def local(three_index, *rest):
    whole_rows = three_index.shape[1] == ROWS
    return (local_balanced if whole_rows else local_padded)(three_index, *rest)


def solution(mesh):
    placed = (
        P(None, "row", "grp"),
        P("grp", None, None),
        P("grp", None, None),
        P("grp", None),
        P("grp"),
        P(),
    )
    return jax.shard_map(
        local, mesh=mesh, in_specs=placed, out_specs=P(("grp", "row"), None), check_vma=False
    )
```

```python
import functools

import jax
import jax.numpy as jnp
from jax import lax
from jax.experimental import pallas as pl
from jax.experimental.pallas import tpu as pltpu
from jax.sharding import PartitionSpec as P

TILE = 64
SPAN = 5
REACH = 2
LANES = 128
ROWS = 256
FOLD = ROWS // TILE


def pack_kernel(list_ref, occupancy_ref, source_ref, packed_ref):
    count, slots = list_ref.shape
    entries = source_ref.shape[1]
    low_half = lax.broadcasted_iota(jnp.int32, (1, LANES), 1) < TILE

    def pick(group, pair):
        slot = jnp.int32(0)
        found = jnp.int32(0)
        for j in range(slots):
            hit = (list_ref[group, j] == pair) & (j < occupancy_ref[group])
            slot = jnp.where(hit, j, slot)
            found = jnp.where(hit, 1, found)
        return slot, found

    def columns(group):
        return pl.ds(pl.multiple_of((group // 2) * LANES, LANES), LANES)

    def step(index, carry):
        for parity in range(2):
            pair = 2 * index + parity
            for couple in range(2):
                first = lax.rem(pair - 4 + 2 * couple + count, count)
                second = lax.rem(pair - 3 + 2 * couple + count, count)
                low, high = (first, second) if parity == 0 else (second, first)
                low_slot, low_found = pick(low, pair)
                high_slot, high_found = pick(high, pair)
                found = jnp.where(low_half, low_found, high_found) > 0
                value = jnp.where(
                    low_half,
                    source_ref[low_slot, :, columns(low)],
                    source_ref[high_slot, :, columns(high)],
                )
                packed_ref[pair, pl.ds(couple * entries, entries), :] = jnp.where(
                    found, value, jnp.zeros_like(value)
                )
            slot, found = pick(pair, pair)
            value = source_ref[slot, :, columns(pair)]
            value = jnp.where(found > 0, value, jnp.zeros_like(value))
            upper, under = value[: entries // 2], value[entries // 2 :]
            if parity == 0:
                folded = jnp.concatenate([upper[:, :TILE], under[:, :TILE]], axis=1)
            else:
                folded = jnp.concatenate([upper[:, TILE:], under[:, TILE:]], axis=1)
            packed_ref[pair, pl.ds(2 * entries, entries // 2), :] = folded
        return carry

    lax.fori_loop(0, count // 2, step, 0)


def pack(three_index, pair_list, occupancy):
    count = pair_list.shape[0]
    entries = three_index.shape[1]
    return pl.pallas_call(
        pack_kernel,
        out_shape=jax.ShapeDtypeStruct((count, 5 * entries // 2, LANES), jnp.bfloat16),
        in_specs=[
            pl.BlockSpec(memory_space=pltpu.SMEM),
            pl.BlockSpec(memory_space=pltpu.SMEM),
            pl.BlockSpec(memory_space=pltpu.VMEM),
        ],
        out_specs=pl.BlockSpec(memory_space=pltpu.VMEM),
        compiler_params=pltpu.CompilerParams(vmem_limit_bytes=32 * 1024 * 1024),
        name="pack",
    )(pair_list, occupancy, three_index)


def factor_kernel(index_ref, occupied_ref, virtual_ref, left_ref, right_ref):
    row = lax.broadcasted_iota(jnp.int32, (ROWS, ROWS), 0)
    column = lax.broadcasted_iota(jnp.int32, (ROWS, ROWS), 1)
    spread = (
        lax.broadcasted_iota(jnp.int32, (ROWS, TILE), 0) // FOLD
        == lax.broadcasted_iota(jnp.int32, (ROWS, TILE), 1)
    ).astype(jnp.bfloat16)
    block = lax.dot_general(
        spread, virtual_ref[0], (((1,), (1,)), ((), ())), preferred_element_type=jnp.float32
    )
    block = jnp.concatenate([block] * FOLD, axis=1)
    right_ref[...] = jnp.where(row % FOLD == column // TILE, block, 0.0).astype(jnp.bfloat16)
    entry = lax.broadcasted_iota(jnp.int32, (TILE, ROWS), 1)
    spread = (
        (entry // (FOLD * FOLD)) * FOLD + entry % FOLD
        == lax.broadcasted_iota(jnp.int32, (TILE, ROWS), 0)
    ).astype(jnp.bfloat16)
    block = lax.dot_general(
        occupied_ref[0], spread, (((0,), (0,)), ((), ())), preferred_element_type=jnp.float32
    )
    block = jnp.concatenate([block] * FOLD, axis=0)
    left_ref[...] = jnp.where(row // TILE == (column // FOLD) % FOLD, block, 0.0).astype(
        jnp.bfloat16
    )


def factors(blocks, occupied_factor, virtual_factor):
    shape = jax.ShapeDtypeStruct((ROWS, ROWS), jnp.bfloat16)
    whole = pl.BlockSpec((ROWS, ROWS), lambda i, index: (0, 0))
    return pl.pallas_call(
        factor_kernel,
        out_shape=(shape, shape),
        grid_spec=pltpu.PrefetchScalarGridSpec(
            num_scalar_prefetch=1,
            grid=(1,),
            in_specs=[
                pl.BlockSpec((1, TILE, TILE), lambda i, index: (index[0], 0, 0)),
                pl.BlockSpec((1, TILE, TILE), lambda i, index: (index[1], 0, 0)),
            ],
            out_specs=(whole, whole),
        ),
        cost_estimate=pl.CostEstimate(
            flops=4_000_000, bytes_accessed=300_000, transcendentals=0
        ),
        name="factors",
    )(blocks, occupied_factor, virtual_factor)


def gram_kernel(parity_ref, left_ref, right_ref, tiles_ref, *refs):
    outs, half_ref, gram_ref = refs[:SPAN], refs[SPAN], refs[SPAN + 1]
    entries = tiles_ref.shape[1] * 2 // 5
    sources = ROWS // entries
    steps = ROWS // (FOLD * FOLD)
    for block in range(TILE * TILE // ROWS):
        span = pl.ds(block * sources, sources)
        first = tiles_ref[span, pl.ds(0, entries), :].reshape(ROWS, LANES)
        second = tiles_ref[span, pl.ds(entries, entries), :].reshape(ROWS, LANES)
        third = tiles_ref[span, pl.ds(2 * entries, entries // 2), :]
        third = jnp.concatenate([third[..., :TILE], third[..., TILE:]], axis=1)
        values = jnp.concatenate([first, second, third.reshape(ROWS, TILE)], axis=1)
        half = jnp.dot(right_ref[...], values, preferred_element_type=jnp.float32)
        half_ref[block] = half.astype(jnp.bfloat16).reshape(steps, FOLD * FOLD, SPAN * TILE)
    for step in range(steps):
        values = half_ref[:, step].reshape(ROWS, SPAN * TILE)
        panel = jnp.dot(left_ref[...], values, preferred_element_type=jnp.float32)
        panel = panel.astype(jnp.bfloat16)
        part = lax.dot_general(
            panel, panel, (((0,), (0,)), ((), ())), preferred_element_type=jnp.float32
        )
        if step == 0:
            gram_ref[...] = part
        else:
            gram_ref[...] += part
    odd = parity_ref[0] == 1
    scale = 0.5 / TILE
    for place in range(SPAN):
        swapped = place ^ 1 if place < SPAN - 1 else place
        rows = jnp.where(
            odd,
            gram_ref[pl.ds(swapped * TILE, TILE), :],
            gram_ref[pl.ds(place * TILE, TILE), :],
        )
        rows = rows * scale
        pieces = []
        for other in range(max(place - REACH, 0), min(place + REACH, SPAN - 1) + 1):
            turned = other ^ 1 if other < SPAN - 1 else other
            pieces.append(
                jnp.where(
                    odd,
                    rows[:, turned * TILE : (turned + 1) * TILE],
                    rows[:, other * TILE : (other + 1) * TILE],
                )
            )
        outs[place][...] = jnp.concatenate(pieces, axis=1)


def neighbours(place):
    return min(place + REACH, SPAN - 1) - max(place - REACH, 0) + 1


def gram(parity, left, right, tiles):
    vmem = pl.BlockSpec(memory_space=pltpu.VMEM)
    return pl.pallas_call(
        gram_kernel,
        out_shape=tuple(
            jax.ShapeDtypeStruct((TILE, TILE * neighbours(place)), jnp.float32)
            for place in range(SPAN)
        ),
        in_specs=[pl.BlockSpec(memory_space=pltpu.SMEM), vmem, vmem, vmem],
        out_specs=(vmem,) * SPAN,
        scratch_shapes=[
            pltpu.VMEM((TILE * TILE // ROWS, ROWS // (FOLD * FOLD), FOLD * FOLD, SPAN * TILE), jnp.bfloat16),
            pltpu.VMEM((SPAN * TILE, SPAN * TILE), jnp.float32),
        ],
        compiler_params=pltpu.CompilerParams(vmem_limit_bytes=32 * 1024 * 1024),
        name="gram",
    )(parity, left, right, tiles)


CHUNKS = 8
BATCH = 4
CAPACITIES = (26, 28, 30, 36)
ROOM = CAPACITIES[-1]
UNIT = FOLD * FOLD
RECIPROCALS = (4096, 2048, 1366, 1024, 820)


def swap_halves(value):
    return jnp.concatenate([value[:, TILE:], value[:, :TILE]], axis=1)


def plan_tiles(list_ref, occupancy_ref, plan_ref, level_ref):
    slots, count = list_ref.shape
    held, shed = SPAN * count, SPAN * count + count

    for index in range(SPAN * count):
        plan_ref[index] = 0
    for group in range(count):
        for j in range(slots):
            t = list_ref[j, group] - group
            t = jnp.where(t < 0, t + count, t)
            plan_ref[group * SPAN + t] = jnp.where(j < occupancy_ref[group], j + 1, -1)
    entries = [[plan_ref[group * SPAN + t] for t in range(SPAN)] for group in range(count)]

    def quotient(value, factor):
        return (value * factor) >> 12

    heres, factors = [], []
    for pair in range(count):
        here = jnp.int32(0)
        for t in range(SPAN):
            here += jnp.where(entries[(pair - t) % count][t] > 0, 1, 0)
        factor = jnp.int32(RECIPROCALS[-1])
        for d in range(SPAN - 1, 0, -1):
            factor = jnp.where(here <= d, RECIPROCALS[d - 1], factor)
        heres.append(here)
        factors.append(jnp.where(here > 0, factor, 0))
        plan_ref[held + pair] = here
    def shares(capacity):
        gives = [None] * count
        taken = jnp.int32(0)
        for _ in range(2):
            for pair in range(count - 1, -1, -1):
                here = heres[pair]
                excess = jnp.maximum(CHUNKS * here + taken - capacity, 0)
                gives[pair] = jnp.minimum(quotient(excess + here - 1, factors[pair]), CHUNKS)
                taken = here * gives[pair]
        most = jnp.int32(0)
        for pair in range(count):
            after = (pair + 1) % count
            load = heres[pair] * (CHUNKS - gives[pair]) + heres[after] * gives[after]
            most = jnp.maximum(most, load)
        return gives, most <= capacity

    level = jnp.int32(len(CAPACITIES) - 1)
    gives = [jnp.int32(0)] * count
    for index in range(len(CAPACITIES) - 2, -1, -1):
        tried, fits = shares(CAPACITIES[index])
        level = jnp.where(fits, index, level)
        gives = [jnp.where(fits, new, old) for new, old in zip(tried, gives)]
    for pair in range(count):
        plan_ref[shed + pair] = gives[pair]
    level_ref[0] = level

    @pl.when(level == len(CAPACITIES) - 1)
    def _():
        for pair in range(count):
            listed = jnp.int32(0)
            before = jnp.int32(0)
            for t in range(SPAN):
                listed += jnp.where(entries[(pair - t) % count][t] != 0, 1, 0)
            for distance in range(1, SPAN):
                for t in range(distance):
                    before += jnp.where(entries[(pair - distance) % count][t] != 0, 1, 0)
            factor = jnp.int32(RECIPROCALS[-1])
            for d in range(SPAN - 1, 0, -1):
                factor = jnp.where(listed <= d, RECIPROCALS[d - 1], factor)
            give = quotient(CHUNKS * (2 * SPAN - before), factor)
            plan_ref[shed + pair] = jnp.where(listed > 0, give, 0)

    return entries, heres


def source_kernel(
    list_hbm, occupancy_hbm, blocks_hbm, tiles_hbm, virtual_hbm,
    *refs,
):
    outs, refs = refs[: len(CAPACITIES)], refs[len(CAPACITIES) :]
    plan_ref, level_ref, list_ref, occupancy_ref, blocks_ref, *refs = refs
    tiles_ref, virtual_ref, packed_ref, small_sem, virtual_sem, in_sem, out_sem = refs
    count = list_ref.shape[1]
    shed = SPAN * count + count
    parts = count // 4
    width = 4 * TILE
    small = [
        pltpu.make_async_copy(there, here, small_sem.at[index])
        for index, (there, here) in enumerate(
            ((blocks_hbm, blocks_ref), (list_hbm, list_ref), (occupancy_hbm, occupancy_ref))
        )
    ]
    for copy in small:
        copy.start()
    fetches = []
    for part in range(parts):
        lanes = pl.ds(part * width, width)
        fetches.append(
            pltpu.make_async_copy(
                tiles_hbm.at[:, :, lanes], tiles_ref.at[:, :, lanes], in_sem.at[part]
            )
        )
    for copy in fetches:
        copy.start()
    small[0].wait()
    picks = []
    for pair in range(count):
        picks.append(
            pltpu.make_async_copy(
                virtual_hbm.at[blocks_ref[1, pair]], virtual_ref.at[pair], virtual_sem.at[pair]
            )
        )
        picks[-1].start()
    small[1].wait()
    small[2].wait()
    entries, heres = plan_tiles(list_ref, occupancy_ref, plan_ref, level_ref)
    gives = [plan_ref[shed + pair] for pair in range(count)]
    for copy in picks:
        copy.wait()

    low = lax.broadcasted_iota(jnp.int32, (1, LANES), 1) < TILE
    spread = (
        lax.broadcasted_iota(jnp.int32, (ROWS, TILE), 0) // FOLD
        == lax.broadcasted_iota(jnp.int32, (ROWS, TILE), 1)
    ).astype(jnp.bfloat16)
    diagonal = (
        lax.broadcasted_iota(jnp.int32, (ROWS, ROWS), 0) % FOLD
        == lax.broadcasted_iota(jnp.int32, (ROWS, ROWS), 1) // TILE
    ).astype(jnp.bfloat16)

    level = level_ref[0]

    def send(dests, act):
        for index, capacity in enumerate(CAPACITIES):

            @pl.when(level == index)
            def _(index=index, capacity=capacity):
                for dest in dests:
                    held = packed_ref.at[pl.ds(dest * (ROOM + 1), capacity)]
                    copy = pltpu.make_async_copy(held, outs[index].at[dest], out_sem.at[dest])
                    copy.start() if act else copy.wait()

    arrived = set()
    rights = {}
    written = set()
    sent = []
    started = 0
    for index in range(count):
        pair = (index + 4) % count
        previous = (pair - 1) % count
        for t in range(SPAN):
            part = ((pair - t) % count) // 4
            if part not in arrived:
                arrived.add(part)
                fetches[part].wait()
        if pair not in rights:
            couple = pair // 2 * 2
            block = lax.dot_general(
                spread,
                virtual_ref[couple : couple + 2].reshape(2 * TILE, TILE),
                (((1,), (1,)), ((), ())),
                preferred_element_type=jnp.float32,
            ).astype(jnp.bfloat16)
            turned = swap_halves(block)
            for side in range(2):
                double = jnp.where(low, turned, block) if side else jnp.where(low, block, turned)
                rights[couple + side] = jnp.concatenate([double, double], axis=1) * diagonal
        values, ranks = [], []
        rank = jnp.int32(0)
        for place in range(SPAN):
            t = SPAN - 1 - place
            group = (pair - t) % count
            entry = entries[group][t]
            columns = pl.ds((group // 2) * LANES, LANES)
            values.append(tiles_ref[jnp.maximum(entry - 1, 0), :, columns])
            ranks.append((entry > 0, rank))
            rank += jnp.where(entry > 0, 1, 0)
        parity = pair % 2
        lows = [values[place] for place in range(parity, SPAN, 2)]
        highs = [values[place] for place in range(1 - parity, SPAN, 2)]
        if parity == 0:
            highs.append(lows[-1])
        else:
            lows.append(highs[-1])
        joined = [jnp.where(low, a, b) for a, b in zip(lows, highs)]
        half = jnp.dot(
            rights[pair], jnp.concatenate(joined, axis=1), preferred_element_type=jnp.float32
        ).astype(jnp.bfloat16)
        here, give = heres[pair], gives[pair]
        base = previous * (ROOM + 1) + heres[previous] * (CHUNKS - gives[previous])
        starts = []
        for chunk in range(CHUNKS):
            starts.append(
                jnp.where(
                    chunk >= give,
                    pair * (ROOM + 1) + (chunk - give) * here,
                    base + chunk * here,
                )
            )
        middle = ROWS // 2
        for place in range(SPAN):
            piece = half[:, (place // 2) * LANES : (place // 2 + 1) * LANES]
            if (place + parity) % 2 == 0:
                folded = jnp.where(low, piece[:middle], swap_halves(piece[middle:]))
            else:
                folded = jnp.where(low, swap_halves(piece[:middle]), piece[middle:])
            found, rank = ranks[place]
            for chunk in range(CHUNKS):
                slot = jnp.where(found, starts[chunk] + rank, count * (ROOM + 1))
                packed_ref[slot] = folded[chunk * UNIT : (chunk + 1) * UNIT]
        written.add(pair)
        for dest in (pair, previous):
            if dest in written and (dest + 1) % count in written and dest not in sent:
                sent.append(dest)
        if index % BATCH == BATCH - 1:
            send(sent[started:], True)
            started = len(sent)
    send(sent, False)


def source(three_index, virtual_factor, pair_list, occupancy, pair_blocks):
    count = pair_list.shape[0]
    smem = pl.BlockSpec(memory_space=pltpu.SMEM)
    hbm = pl.BlockSpec(memory_space=pltpu.HBM)
    return pl.pallas_call(
        source_kernel,
        out_shape=(
            *(
                jax.ShapeDtypeStruct((count, capacity, UNIT, LANES), jnp.bfloat16)
                for capacity in CAPACITIES
            ),
            jax.ShapeDtypeStruct(((SPAN + 2) * count,), jnp.int32),
            jax.ShapeDtypeStruct((1,), jnp.int32),
        ),
        in_specs=[hbm] * 5,
        out_specs=(hbm,) * len(CAPACITIES) + (smem, smem),
        scratch_shapes=[
            pltpu.SMEM(pair_list.shape[::-1], jnp.int32),
            pltpu.SMEM(occupancy.shape, jnp.int32),
            pltpu.SMEM(pair_blocks.shape[::-1], jnp.int32),
            pltpu.VMEM(three_index.shape, jnp.bfloat16),
            pltpu.VMEM((count,) + virtual_factor.shape[1:], jnp.bfloat16),
            pltpu.VMEM((count * (ROOM + 1) + 1, UNIT, LANES), jnp.bfloat16),
            pltpu.SemaphoreType.DMA((3,)),
            pltpu.SemaphoreType.DMA((count,)),
            pltpu.SemaphoreType.DMA((count // 4,)),
            pltpu.SemaphoreType.DMA((count,)),
        ],
        compiler_params=pltpu.CompilerParams(vmem_limit_bytes=60 * 1024 * 1024),
        name="source",
    )(pair_list.T, occupancy, pair_blocks.T, three_index, virtual_factor)


def left_kernel(own_ref, blocks_hbm, occupied_hbm, left_ref, blocks_ref, occupied_ref, sem):
    count = blocks_ref.shape[1]
    fetch = pltpu.make_async_copy(blocks_hbm, blocks_ref, sem.at[0])
    fetch.start()
    fetch.wait()
    copies = []
    for segment in range(2):
        pair = own_ref[0] + segment
        pair = jnp.where(pair >= count, pair - count, pair)
        copies.append(
            pltpu.make_async_copy(
                occupied_hbm.at[blocks_ref[0, pair]], occupied_ref.at[segment], sem.at[segment + 1]
            )
        )
        copies[-1].start()
    row = lax.broadcasted_iota(jnp.int32, (ROWS, ROWS), 0)
    column = lax.broadcasted_iota(jnp.int32, (ROWS, ROWS), 1)
    entry = lax.broadcasted_iota(jnp.int32, (TILE, ROWS), 1)
    spread = (
        (entry // UNIT) * FOLD + entry % FOLD
        == lax.broadcasted_iota(jnp.int32, (TILE, ROWS), 0)
    ).astype(jnp.bfloat16)
    for segment in range(2):
        copies[segment].wait()
        block = lax.dot_general(
            occupied_ref[segment],
            spread,
            (((0,), (0,)), ((), ())),
            preferred_element_type=jnp.float32,
        )
        block = jnp.concatenate([block] * FOLD, axis=0)
        left_ref[segment] = jnp.where(
            row // TILE == (column // FOLD) % FOLD, block, 0.0
        ).astype(jnp.bfloat16)


def left_factors(own, pair_blocks, occupied_factor):
    hbm = pl.BlockSpec(memory_space=pltpu.HBM)
    return pl.pallas_call(
        left_kernel,
        out_shape=jax.ShapeDtypeStruct((2, ROWS, ROWS), jnp.bfloat16),
        in_specs=[pl.BlockSpec(memory_space=pltpu.SMEM), hbm, hbm],
        out_specs=pl.BlockSpec(memory_space=pltpu.VMEM),
        scratch_shapes=[
            pltpu.SMEM(pair_blocks.shape[::-1], jnp.int32),
            pltpu.VMEM((2,) + occupied_factor.shape[1:], jnp.bfloat16),
            pltpu.SemaphoreType.DMA((3,)),
        ],
        cost_estimate=pl.CostEstimate(
            flops=4_000_000, bytes_accessed=300_000, transcendentals=0
        ),
        compiler_params=pltpu.CompilerParams(vmem_limit_bytes=16 * 1024 * 1024),
        name="left_factors",
    )(own, pair_blocks.T, occupied_factor)


WIDE = SPAN + 1
UNROLL = 2


def shared_kernel(own_ref, plan_ref, left_ref, tiles_ref, *refs):
    outs, first_ref, rest_ref = refs[:WIDE], refs[WIDE], refs[WIDE + 1]
    count, capacity = tiles_ref.shape[:2]
    held, shed = SPAN * count, SPAN * count + count
    own = own_ref[0]
    after = jnp.where(own == count - 1, 0, own + 1)
    rows_with_rows = (((1,), (1,)), ((), ()))
    first_ref[...] = jnp.zeros_like(first_ref)
    rest_ref[...] = jnp.zeros_like(rest_ref)

    def tiles_of(pair, shift):
        found, ranks = [False] * WIDE, [0] * WIDE
        rank = jnp.int32(0)
        for place in range(SPAN):
            t = SPAN - 1 - place
            group = pair - t
            group = jnp.where(group < 0, group + count, group)
            found[place + shift] = plan_ref[group * SPAN + t] > 0
            ranks[place + shift] = rank
            rank += jnp.where(found[place + shift], 1, 0)
        return found, ranks

    own_here, after_here = plan_ref[held + own], plan_ref[held + after]
    own_units = CHUNKS - plan_ref[shed + own]
    units = own_units + plan_ref[shed + after]
    own_found, own_ranks = tiles_of(own, 0)
    after_found, after_ranks = tiles_of(after, 1)

    def gather(index):
        second = index >= own_units
        here = jnp.where(second, after_here, own_here)
        base = jnp.where(second, own_units * own_here, 0)
        base += jnp.where(second, index - own_units, index) * here
        values = []
        for place in range(WIDE):
            found = jnp.where(second, after_found[place], own_found[place])
            found = found & (index < units)
            slot = base + jnp.where(second, after_ranks[place], own_ranks[place])
            slot = jnp.where(found, slot, 0)
            value = tiles_ref[:, jnp.minimum(slot, capacity - 1)]
            value = jnp.where(found, value, jnp.zeros_like(value))
            values.append(value.reshape(ROWS, LANES))
        return lax.dot_general(
            jnp.concatenate(values, axis=1).T,
            left_ref[jnp.where(second, 1, 0)],
            rows_with_rows,
            preferred_element_type=jnp.float32,
        ).astype(jnp.bfloat16)

    def step(index, carry):
        for inner in range(UNROLL):
            panel = gather(UNROLL * index + inner).reshape(WIDE, 2, TILE, ROWS)
            stack = jnp.concatenate(
                [panel[:, half].reshape(WIDE * TILE, ROWS) for half in range(2)], axis=1
            )
            first = stack[:LANES]
            first_ref[...] += lax.dot_general(
                first, first, rows_with_rows, preferred_element_type=jnp.float32
            )
            rest_ref[...] += lax.dot_general(
                stack, stack[LANES:], rows_with_rows, preferred_element_type=jnp.float32
            )
        return carry

    lax.fori_loop(0, (units + UNROLL - 1) // UNROLL, step, 0)

    turned = rest_ref[pl.ds(0, LANES), :][:, :LANES].T
    scale = 0.5 / TILE
    for place in range(WIDE):
        rows = rest_ref[pl.ds(place * TILE, TILE), :]
        if place < 2:
            left = first_ref[pl.ds(place * TILE, TILE), :]
        else:
            left = turned[(place - 2) * TILE : (place - 1) * TILE] if place < 4 else rows[:, :LANES]
        rows = jnp.concatenate([left, rows], axis=1)
        first, last = max(place - REACH, 0), min(place + REACH, WIDE - 1)
        outs[place][...] = rows[:, first * TILE : (last + 1) * TILE] * scale


def shared_gram(own, plan, left, tiles):
    vmem = pl.BlockSpec(memory_space=pltpu.VMEM)
    smem = pl.BlockSpec(memory_space=pltpu.SMEM)
    widths = [
        TILE * (min(place + REACH, WIDE - 1) - max(place - REACH, 0) + 1) for place in range(WIDE)
    ]
    return pl.pallas_call(
        shared_kernel,
        out_shape=tuple(jax.ShapeDtypeStruct((TILE, width), jnp.float32) for width in widths),
        in_specs=[smem, smem, vmem, vmem],
        out_specs=(vmem,) * WIDE,
        scratch_shapes=[
            pltpu.VMEM((LANES, LANES), jnp.float32),
            pltpu.VMEM((WIDE * TILE, WIDE * TILE - LANES), jnp.float32),
        ],
        compiler_params=pltpu.CompilerParams(vmem_limit_bytes=32 * 1024 * 1024),
        name="shared_gram",
    )(own, plan, left, tiles)


def assemble(parts, shifts, count):
    total = None
    for place, (part, shift) in enumerate(zip(parts, shifts)):
        if shift:
            part = lax.ppermute(
                part, "row", [(device, (device + shift) % count) for device in range(count)]
            )
        before = max(REACH - place, 0) * TILE
        after = (2 * REACH + 1) * TILE - before - part.shape[1]
        part = jnp.pad(part, ((0, 0), (before, after)))
        total = part if total is None else total + part
    return total


def exchange(value):
    return lax.all_to_all(value, "row", split_axis=0, concat_axis=0, tiled=True)


def local_balanced(
    three_index, occupied_factor, virtual_factor, pair_list, occupancy, pair_blocks
):
    count = lax.axis_size("row")
    own = lax.axis_index("row")
    *packed, plan, level = source(
        three_index, virtual_factor, pair_list, occupancy, pair_blocks
    )
    own = own.reshape(1).astype(jnp.int32)

    def at_level(index):
        def run(packed):
            tiles = exchange(packed[index])
            left = left_factors(own, pair_blocks, occupied_factor)
            return shared_gram(own, plan, left, tiles)

        return run

    parts = lax.switch(level[0], [at_level(index) for index in range(len(packed))], packed)
    return assemble(parts, range(1 - SPAN, 2), count)


def local_padded(three_index, occupied_factor, virtual_factor, pair_list, occupancy, pair_blocks):
    count = lax.axis_size("row")
    own = lax.axis_index("row")
    packed = pack(three_index, pair_list, occupancy)
    tiles = exchange(packed)
    blocks = lax.dynamic_index_in_dim(pair_blocks, own, 0, keepdims=False)
    left, right = factors(blocks, occupied_factor, virtual_factor)
    parity = lax.rem(own, 2).reshape(1).astype(jnp.int32)
    parts = gram(parity, left, right, tiles)
    return assemble(parts, range(1 - SPAN, 1), count)


def local(three_index, *rest):
    whole_rows = three_index.shape[1] == ROWS
    return (local_balanced if whole_rows else local_padded)(three_index, *rest)


def solution(mesh):
    placed = (
        P(None, "row", "grp"),
        P("grp", None, None),
        P("grp", None, None),
        P("grp", None),
        P("grp"),
        P(),
    )
    return jax.shard_map(
        local, mesh=mesh, in_specs=placed, out_specs=P(("grp", "row"), None), check_vma=False
    )
```

```python
import functools

import jax
import jax.numpy as jnp
from jax import lax
from jax.experimental import pallas as pl
from jax.experimental.pallas import tpu as pltpu
from jax.sharding import PartitionSpec as P

TILE = 64
SPAN = 5
REACH = 2
LANES = 128
ROWS = 256
FOLD = ROWS // TILE


def pack_kernel(list_ref, occupancy_ref, source_ref, packed_ref):
    count, slots = list_ref.shape
    entries = source_ref.shape[1]
    low_half = lax.broadcasted_iota(jnp.int32, (1, LANES), 1) < TILE

    def pick(group, pair):
        slot = jnp.int32(0)
        found = jnp.int32(0)
        for j in range(slots):
            hit = (list_ref[group, j] == pair) & (j < occupancy_ref[group])
            slot = jnp.where(hit, j, slot)
            found = jnp.where(hit, 1, found)
        return slot, found

    def columns(group):
        return pl.ds(pl.multiple_of((group // 2) * LANES, LANES), LANES)

    def step(index, carry):
        for parity in range(2):
            pair = 2 * index + parity
            for couple in range(2):
                first = lax.rem(pair - 4 + 2 * couple + count, count)
                second = lax.rem(pair - 3 + 2 * couple + count, count)
                low, high = (first, second) if parity == 0 else (second, first)
                low_slot, low_found = pick(low, pair)
                high_slot, high_found = pick(high, pair)
                found = jnp.where(low_half, low_found, high_found) > 0
                value = jnp.where(
                    low_half,
                    source_ref[low_slot, :, columns(low)],
                    source_ref[high_slot, :, columns(high)],
                )
                packed_ref[pair, pl.ds(couple * entries, entries), :] = jnp.where(
                    found, value, jnp.zeros_like(value)
                )
            slot, found = pick(pair, pair)
            value = source_ref[slot, :, columns(pair)]
            value = jnp.where(found > 0, value, jnp.zeros_like(value))
            upper, under = value[: entries // 2], value[entries // 2 :]
            if parity == 0:
                folded = jnp.concatenate([upper[:, :TILE], under[:, :TILE]], axis=1)
            else:
                folded = jnp.concatenate([upper[:, TILE:], under[:, TILE:]], axis=1)
            packed_ref[pair, pl.ds(2 * entries, entries // 2), :] = folded
        return carry

    lax.fori_loop(0, count // 2, step, 0)


def pack(three_index, pair_list, occupancy):
    count = pair_list.shape[0]
    entries = three_index.shape[1]
    return pl.pallas_call(
        pack_kernel,
        out_shape=jax.ShapeDtypeStruct((count, 5 * entries // 2, LANES), jnp.bfloat16),
        in_specs=[
            pl.BlockSpec(memory_space=pltpu.SMEM),
            pl.BlockSpec(memory_space=pltpu.SMEM),
            pl.BlockSpec(memory_space=pltpu.VMEM),
        ],
        out_specs=pl.BlockSpec(memory_space=pltpu.VMEM),
        compiler_params=pltpu.CompilerParams(vmem_limit_bytes=32 * 1024 * 1024),
        name="pack",
    )(pair_list, occupancy, three_index)


def factor_kernel(index_ref, occupied_ref, virtual_ref, left_ref, right_ref):
    row = lax.broadcasted_iota(jnp.int32, (ROWS, ROWS), 0)
    column = lax.broadcasted_iota(jnp.int32, (ROWS, ROWS), 1)
    spread = (
        lax.broadcasted_iota(jnp.int32, (ROWS, TILE), 0) // FOLD
        == lax.broadcasted_iota(jnp.int32, (ROWS, TILE), 1)
    ).astype(jnp.bfloat16)
    block = lax.dot_general(
        spread, virtual_ref[0], (((1,), (1,)), ((), ())), preferred_element_type=jnp.float32
    )
    block = jnp.concatenate([block] * FOLD, axis=1)
    right_ref[...] = jnp.where(row % FOLD == column // TILE, block, 0.0).astype(jnp.bfloat16)
    entry = lax.broadcasted_iota(jnp.int32, (TILE, ROWS), 1)
    spread = (
        (entry // (FOLD * FOLD)) * FOLD + entry % FOLD
        == lax.broadcasted_iota(jnp.int32, (TILE, ROWS), 0)
    ).astype(jnp.bfloat16)
    block = lax.dot_general(
        occupied_ref[0], spread, (((0,), (0,)), ((), ())), preferred_element_type=jnp.float32
    )
    block = jnp.concatenate([block] * FOLD, axis=0)
    left_ref[...] = jnp.where(row // TILE == (column // FOLD) % FOLD, block, 0.0).astype(
        jnp.bfloat16
    )


def factors(blocks, occupied_factor, virtual_factor):
    shape = jax.ShapeDtypeStruct((ROWS, ROWS), jnp.bfloat16)
    whole = pl.BlockSpec((ROWS, ROWS), lambda i, index: (0, 0))
    return pl.pallas_call(
        factor_kernel,
        out_shape=(shape, shape),
        grid_spec=pltpu.PrefetchScalarGridSpec(
            num_scalar_prefetch=1,
            grid=(1,),
            in_specs=[
                pl.BlockSpec((1, TILE, TILE), lambda i, index: (index[0], 0, 0)),
                pl.BlockSpec((1, TILE, TILE), lambda i, index: (index[1], 0, 0)),
            ],
            out_specs=(whole, whole),
        ),
        cost_estimate=pl.CostEstimate(
            flops=4_000_000, bytes_accessed=300_000, transcendentals=0
        ),
        name="factors",
    )(blocks, occupied_factor, virtual_factor)


def gram_kernel(parity_ref, left_ref, right_ref, tiles_ref, *refs):
    outs, half_ref, gram_ref = refs[:SPAN], refs[SPAN], refs[SPAN + 1]
    entries = tiles_ref.shape[1] * 2 // 5
    sources = ROWS // entries
    steps = ROWS // (FOLD * FOLD)
    for block in range(TILE * TILE // ROWS):
        span = pl.ds(block * sources, sources)
        first = tiles_ref[span, pl.ds(0, entries), :].reshape(ROWS, LANES)
        second = tiles_ref[span, pl.ds(entries, entries), :].reshape(ROWS, LANES)
        third = tiles_ref[span, pl.ds(2 * entries, entries // 2), :]
        third = jnp.concatenate([third[..., :TILE], third[..., TILE:]], axis=1)
        values = jnp.concatenate([first, second, third.reshape(ROWS, TILE)], axis=1)
        half = jnp.dot(right_ref[...], values, preferred_element_type=jnp.float32)
        half_ref[block] = half.astype(jnp.bfloat16).reshape(steps, FOLD * FOLD, SPAN * TILE)
    for step in range(steps):
        values = half_ref[:, step].reshape(ROWS, SPAN * TILE)
        panel = jnp.dot(left_ref[...], values, preferred_element_type=jnp.float32)
        panel = panel.astype(jnp.bfloat16)
        part = lax.dot_general(
            panel, panel, (((0,), (0,)), ((), ())), preferred_element_type=jnp.float32
        )
        if step == 0:
            gram_ref[...] = part
        else:
            gram_ref[...] += part
    odd = parity_ref[0] == 1
    scale = 0.5 / TILE
    for place in range(SPAN):
        swapped = place ^ 1 if place < SPAN - 1 else place
        rows = jnp.where(
            odd,
            gram_ref[pl.ds(swapped * TILE, TILE), :],
            gram_ref[pl.ds(place * TILE, TILE), :],
        )
        rows = rows * scale
        pieces = []
        for other in range(max(place - REACH, 0), min(place + REACH, SPAN - 1) + 1):
            turned = other ^ 1 if other < SPAN - 1 else other
            pieces.append(
                jnp.where(
                    odd,
                    rows[:, turned * TILE : (turned + 1) * TILE],
                    rows[:, other * TILE : (other + 1) * TILE],
                )
            )
        outs[place][...] = jnp.concatenate(pieces, axis=1)


def neighbours(place):
    return min(place + REACH, SPAN - 1) - max(place - REACH, 0) + 1


def gram(parity, left, right, tiles):
    vmem = pl.BlockSpec(memory_space=pltpu.VMEM)
    return pl.pallas_call(
        gram_kernel,
        out_shape=tuple(
            jax.ShapeDtypeStruct((TILE, TILE * neighbours(place)), jnp.float32)
            for place in range(SPAN)
        ),
        in_specs=[pl.BlockSpec(memory_space=pltpu.SMEM), vmem, vmem, vmem],
        out_specs=(vmem,) * SPAN,
        scratch_shapes=[
            pltpu.VMEM((TILE * TILE // ROWS, ROWS // (FOLD * FOLD), FOLD * FOLD, SPAN * TILE), jnp.bfloat16),
            pltpu.VMEM((SPAN * TILE, SPAN * TILE), jnp.float32),
        ],
        compiler_params=pltpu.CompilerParams(vmem_limit_bytes=32 * 1024 * 1024),
        name="gram",
    )(parity, left, right, tiles)


CHUNKS = 8
BATCH = 2
CAPACITIES = (26, 28, 30, 36)
ROOM = CAPACITIES[-1]
UNIT = FOLD * FOLD
RECIPROCALS = (4096, 2048, 1366, 1024, 820)


def swap_halves(value):
    return jnp.concatenate([value[:, TILE:], value[:, :TILE]], axis=1)


def plan_tiles(list_ref, occupancy_ref, plan_ref, level_ref):
    slots, count = list_ref.shape
    held, shed = SPAN * count, SPAN * count + count

    for index in range(SPAN * count):
        plan_ref[index] = 0
    for group in range(count):
        for j in range(slots):
            t = list_ref[j, group] - group
            t = jnp.where(t < 0, t + count, t)
            plan_ref[group * SPAN + t] = jnp.where(j < occupancy_ref[group], j + 1, -1)
    entries = [[plan_ref[group * SPAN + t] for t in range(SPAN)] for group in range(count)]

    def quotient(value, factor):
        return (value * factor) >> 12

    heres, factors = [], []
    for pair in range(count):
        here = jnp.int32(0)
        for t in range(SPAN):
            here += jnp.where(entries[(pair - t) % count][t] > 0, 1, 0)
        factor = jnp.int32(RECIPROCALS[-1])
        for d in range(SPAN - 1, 0, -1):
            factor = jnp.where(here <= d, RECIPROCALS[d - 1], factor)
        heres.append(here)
        factors.append(jnp.where(here > 0, factor, 0))
        plan_ref[held + pair] = here
    def shares(capacity):
        gives = [None] * count
        taken = jnp.int32(0)
        for _ in range(2):
            for pair in range(count - 1, -1, -1):
                here = heres[pair]
                excess = jnp.maximum(CHUNKS * here + taken - capacity, 0)
                gives[pair] = jnp.minimum(quotient(excess + here - 1, factors[pair]), CHUNKS)
                taken = here * gives[pair]
        most = jnp.int32(0)
        for pair in range(count):
            after = (pair + 1) % count
            load = heres[pair] * (CHUNKS - gives[pair]) + heres[after] * gives[after]
            most = jnp.maximum(most, load)
        return gives, most <= capacity

    level = jnp.int32(len(CAPACITIES) - 1)
    gives = [jnp.int32(0)] * count
    for index in range(len(CAPACITIES) - 2, -1, -1):
        tried, fits = shares(CAPACITIES[index])
        level = jnp.where(fits, index, level)
        gives = [jnp.where(fits, new, old) for new, old in zip(tried, gives)]
    for pair in range(count):
        plan_ref[shed + pair] = gives[pair]
    level_ref[0] = level

    @pl.when(level == len(CAPACITIES) - 1)
    def _():
        for pair in range(count):
            listed = jnp.int32(0)
            before = jnp.int32(0)
            for t in range(SPAN):
                listed += jnp.where(entries[(pair - t) % count][t] != 0, 1, 0)
            for distance in range(1, SPAN):
                for t in range(distance):
                    before += jnp.where(entries[(pair - distance) % count][t] != 0, 1, 0)
            factor = jnp.int32(RECIPROCALS[-1])
            for d in range(SPAN - 1, 0, -1):
                factor = jnp.where(listed <= d, RECIPROCALS[d - 1], factor)
            give = quotient(CHUNKS * (2 * SPAN - before), factor)
            plan_ref[shed + pair] = jnp.where(listed > 0, give, 0)

    return entries, heres


def source_kernel(
    list_hbm, occupancy_hbm, blocks_hbm, tiles_hbm, virtual_hbm,
    *refs,
):
    outs, refs = refs[: len(CAPACITIES)], refs[len(CAPACITIES) :]
    plan_ref, level_ref, list_ref, occupancy_ref, blocks_ref, *refs = refs
    tiles_ref, virtual_ref, right_ref, packed_ref, small_sem, virtual_sem, in_sem, out_sem = refs
    count = list_ref.shape[1]
    shed = SPAN * count + count
    parts = count // 4
    width = 4 * TILE
    small = [
        pltpu.make_async_copy(there, here, small_sem.at[index])
        for index, (there, here) in enumerate(
            ((blocks_hbm, blocks_ref), (list_hbm, list_ref), (occupancy_hbm, occupancy_ref))
        )
    ]
    for copy in small:
        copy.start()
    fetches = []
    for part in range(parts):
        lanes = pl.ds(part * width, width)
        fetches.append(
            pltpu.make_async_copy(
                tiles_hbm.at[:, :, lanes], tiles_ref.at[:, :, lanes], in_sem.at[part]
            )
        )
    table = pltpu.make_async_copy(virtual_hbm, virtual_ref, virtual_sem.at[0])
    table.start()
    for copy in fetches:
        copy.start()
    small[0].wait()
    small[1].wait()
    small[2].wait()
    table.wait()
    low = lax.broadcasted_iota(jnp.int32, (1, LANES), 1) < TILE
    spread = (
        lax.broadcasted_iota(jnp.int32, (ROWS, TILE), 0) // FOLD
        == lax.broadcasted_iota(jnp.int32, (ROWS, TILE), 1)
    ).astype(jnp.bfloat16)
    diagonal = (
        lax.broadcasted_iota(jnp.int32, (ROWS, ROWS), 0) % FOLD
        == lax.broadcasted_iota(jnp.int32, (ROWS, ROWS), 1) // TILE
    ).astype(jnp.bfloat16)
    for couple in range(0, count, 2):
        chosen = [virtual_ref[blocks_ref[1, couple + side]] for side in range(2)]
        block = lax.dot_general(
            spread,
            jnp.concatenate(chosen, axis=0),
            (((1,), (1,)), ((), ())),
            preferred_element_type=jnp.float32,
        ).astype(jnp.bfloat16)
        turned = swap_halves(block)
        for side in range(2):
            double = jnp.where(low, turned, block) if side else jnp.where(low, block, turned)
            right_ref[couple + side] = jnp.concatenate([double, double], axis=1) * diagonal
    entries, heres = plan_tiles(list_ref, occupancy_ref, plan_ref, level_ref)
    gives = [plan_ref[shed + pair] for pair in range(count)]
    level = level_ref[0]

    def send(dests, act):
        for index, capacity in enumerate(CAPACITIES):

            @pl.when(level == index)
            def _(index=index, capacity=capacity):
                for dest in dests:
                    held = packed_ref.at[pl.ds(dest * (ROOM + 1), capacity)]
                    copy = pltpu.make_async_copy(held, outs[index].at[dest], out_sem.at[dest])
                    copy.start() if act else copy.wait()

    arrived = set()
    written = set()
    sent = []
    started = 0
    for index in range(count):
        pair = (index + 4) % count
        previous = (pair - 1) % count
        for t in range(SPAN):
            part = ((pair - t) % count) // 4
            if part not in arrived:
                arrived.add(part)
                fetches[part].wait()
        values, ranks = [], []
        rank = jnp.int32(0)
        for place in range(SPAN):
            t = SPAN - 1 - place
            group = (pair - t) % count
            entry = entries[group][t]
            columns = pl.ds((group // 2) * LANES, LANES)
            values.append(tiles_ref[jnp.maximum(entry - 1, 0), :, columns])
            ranks.append((entry > 0, rank))
            rank += jnp.where(entry > 0, 1, 0)
        parity = pair % 2
        lows = [values[place] for place in range(parity, SPAN, 2)]
        highs = [values[place] for place in range(1 - parity, SPAN, 2)]
        if parity == 0:
            highs.append(lows[-1])
        else:
            lows.append(highs[-1])
        joined = [jnp.where(low, a, b) for a, b in zip(lows, highs)]
        half = jnp.dot(
            right_ref[pair], jnp.concatenate(joined, axis=1), preferred_element_type=jnp.float32
        ).astype(jnp.bfloat16)
        here, give = heres[pair], gives[pair]
        base = previous * (ROOM + 1) + heres[previous] * (CHUNKS - gives[previous])
        starts = []
        for chunk in range(CHUNKS):
            starts.append(
                jnp.where(
                    chunk >= give,
                    pair * (ROOM + 1) + (chunk - give) * here,
                    base + chunk * here,
                )
            )
        middle = ROWS // 2
        for place in range(SPAN):
            piece = half[:, (place // 2) * LANES : (place // 2 + 1) * LANES]
            if (place + parity) % 2 == 0:
                folded = jnp.where(low, piece[:middle], swap_halves(piece[middle:]))
            else:
                folded = jnp.where(low, swap_halves(piece[:middle]), piece[middle:])
            found, rank = ranks[place]
            for chunk in range(CHUNKS):
                slot = jnp.where(found, starts[chunk] + rank, count * (ROOM + 1))
                packed_ref[slot] = folded[chunk * UNIT : (chunk + 1) * UNIT]
        written.add(pair)
        for dest in (pair, previous):
            if dest in written and (dest + 1) % count in written and dest not in sent:
                sent.append(dest)
        if index % BATCH == BATCH - 1:
            send(sent[started:], True)
            started = len(sent)
    send(sent, False)


def source(three_index, virtual_factor, pair_list, occupancy, pair_blocks):
    count = pair_list.shape[0]
    smem = pl.BlockSpec(memory_space=pltpu.SMEM)
    hbm = pl.BlockSpec(memory_space=pltpu.HBM)
    return pl.pallas_call(
        source_kernel,
        out_shape=(
            *(
                jax.ShapeDtypeStruct((count, capacity, UNIT, LANES), jnp.bfloat16)
                for capacity in CAPACITIES
            ),
            jax.ShapeDtypeStruct(((SPAN + 2) * count,), jnp.int32),
            jax.ShapeDtypeStruct((1,), jnp.int32),
        ),
        in_specs=[hbm] * 5,
        out_specs=(hbm,) * len(CAPACITIES) + (smem, smem),
        scratch_shapes=[
            pltpu.SMEM(pair_list.shape[::-1], jnp.int32),
            pltpu.SMEM(occupancy.shape, jnp.int32),
            pltpu.SMEM(pair_blocks.shape[::-1], jnp.int32),
            pltpu.VMEM(three_index.shape, jnp.bfloat16),
            pltpu.VMEM(virtual_factor.shape, jnp.bfloat16),
            pltpu.VMEM((count, ROWS, ROWS), jnp.bfloat16),
            pltpu.VMEM((count * (ROOM + 1) + 1, UNIT, LANES), jnp.bfloat16),
            pltpu.SemaphoreType.DMA((3,)),
            pltpu.SemaphoreType.DMA((1,)),
            pltpu.SemaphoreType.DMA((count // 4,)),
            pltpu.SemaphoreType.DMA((count,)),
        ],
        compiler_params=pltpu.CompilerParams(vmem_limit_bytes=60 * 1024 * 1024),
        name="source",
    )(pair_list.T, occupancy, pair_blocks.T, three_index, virtual_factor)


def left_kernel(own_ref, blocks_hbm, occupied_hbm, left_ref, blocks_ref, occupied_ref, sem):
    count = blocks_ref.shape[1]
    fetch = pltpu.make_async_copy(blocks_hbm, blocks_ref, sem.at[0])
    fetch.start()
    fetch.wait()
    copies = []
    for segment in range(2):
        pair = own_ref[0] + segment
        pair = jnp.where(pair >= count, pair - count, pair)
        copies.append(
            pltpu.make_async_copy(
                occupied_hbm.at[blocks_ref[0, pair]], occupied_ref.at[segment], sem.at[segment + 1]
            )
        )
        copies[-1].start()
    row = lax.broadcasted_iota(jnp.int32, (ROWS, ROWS), 0)
    column = lax.broadcasted_iota(jnp.int32, (ROWS, ROWS), 1)
    entry = lax.broadcasted_iota(jnp.int32, (TILE, ROWS), 1)
    spread = (
        (entry // UNIT) * FOLD + entry % FOLD
        == lax.broadcasted_iota(jnp.int32, (TILE, ROWS), 0)
    ).astype(jnp.bfloat16)
    for segment in range(2):
        copies[segment].wait()
        block = lax.dot_general(
            occupied_ref[segment],
            spread,
            (((0,), (0,)), ((), ())),
            preferred_element_type=jnp.float32,
        )
        block = jnp.concatenate([block] * FOLD, axis=0)
        left_ref[segment] = jnp.where(
            row // TILE == (column // FOLD) % FOLD, block, 0.0
        ).astype(jnp.bfloat16)


def left_factors(own, pair_blocks, occupied_factor):
    hbm = pl.BlockSpec(memory_space=pltpu.HBM)
    return pl.pallas_call(
        left_kernel,
        out_shape=jax.ShapeDtypeStruct((2, ROWS, ROWS), jnp.bfloat16),
        in_specs=[pl.BlockSpec(memory_space=pltpu.SMEM), hbm, hbm],
        out_specs=pl.BlockSpec(memory_space=pltpu.VMEM),
        scratch_shapes=[
            pltpu.SMEM(pair_blocks.shape[::-1], jnp.int32),
            pltpu.VMEM((2,) + occupied_factor.shape[1:], jnp.bfloat16),
            pltpu.SemaphoreType.DMA((3,)),
        ],
        cost_estimate=pl.CostEstimate(
            flops=4_000_000, bytes_accessed=300_000, transcendentals=0
        ),
        compiler_params=pltpu.CompilerParams(vmem_limit_bytes=16 * 1024 * 1024),
        name="left_factors",
    )(own, pair_blocks.T, occupied_factor)


WIDE = SPAN + 1
UNROLL = 3


def shared_kernel(own_ref, plan_ref, left_ref, tiles_ref, *refs):
    outs, first_ref, rest_ref = refs[:WIDE], refs[WIDE], refs[WIDE + 1]
    count, capacity = tiles_ref.shape[:2]
    held, shed = SPAN * count, SPAN * count + count
    own = own_ref[0]
    after = jnp.where(own == count - 1, 0, own + 1)
    rows_with_rows = (((1,), (1,)), ((), ()))
    first_ref[...] = jnp.zeros_like(first_ref)
    rest_ref[...] = jnp.zeros_like(rest_ref)

    def tiles_of(pair, shift):
        found, ranks = [False] * WIDE, [0] * WIDE
        rank = jnp.int32(0)
        for place in range(SPAN):
            t = SPAN - 1 - place
            group = pair - t
            group = jnp.where(group < 0, group + count, group)
            found[place + shift] = plan_ref[group * SPAN + t] > 0
            ranks[place + shift] = rank
            rank += jnp.where(found[place + shift], 1, 0)
        return found, ranks

    own_here, after_here = plan_ref[held + own], plan_ref[held + after]
    own_units = CHUNKS - plan_ref[shed + own]
    units = own_units + plan_ref[shed + after]
    own_found, own_ranks = tiles_of(own, 0)
    after_found, after_ranks = tiles_of(after, 1)

    def gather(index):
        second = index >= own_units
        here = jnp.where(second, after_here, own_here)
        base = jnp.where(second, own_units * own_here, 0)
        base += jnp.where(second, index - own_units, index) * here
        values = []
        for place in range(WIDE):
            found = jnp.where(second, after_found[place], own_found[place])
            found = found & (index < units)
            slot = base + jnp.where(second, after_ranks[place], own_ranks[place])
            slot = jnp.where(found, slot, 0)
            value = tiles_ref[:, jnp.minimum(slot, capacity - 1)]
            value = jnp.where(found, value, jnp.zeros_like(value))
            values.append(value.reshape(ROWS, LANES))
        return lax.dot_general(
            jnp.concatenate(values, axis=1).T,
            left_ref[jnp.where(second, 1, 0)],
            rows_with_rows,
            preferred_element_type=jnp.float32,
        ).astype(jnp.bfloat16)

    def step(index, carry):
        for inner in range(UNROLL):
            panel = gather(UNROLL * index + inner).reshape(WIDE, 2, TILE, ROWS)
            stack = jnp.concatenate(
                [panel[:, half].reshape(WIDE * TILE, ROWS) for half in range(2)], axis=1
            )
            first_ref[...] += lax.dot_general(
                stack[:LANES], stack[: 2 * LANES], rows_with_rows, preferred_element_type=jnp.float32
            )
            rest = stack[LANES:]
            rest_ref[...] += lax.dot_general(
                rest, rest, rows_with_rows, preferred_element_type=jnp.float32
            )
        return carry

    lax.fori_loop(0, (units + UNROLL - 1) // UNROLL, step, 0)

    turned = first_ref[:, LANES:].T
    scale = 0.5 / TILE
    for place in range(WIDE):
        if place < 2:
            rows = first_ref[pl.ds(place * TILE, TILE), :]
        else:
            rows = rest_ref[pl.ds((place - 2) * TILE, TILE), :]
            left = turned[(place - 2) * TILE : (place - 1) * TILE] if place < 4 else rows[:, :LANES]
            rows = jnp.concatenate([left, rows], axis=1)
        first, last = max(place - REACH, 0), min(place + REACH, WIDE - 1)
        outs[place][...] = rows[:, first * TILE : (last + 1) * TILE] * scale


def shared_gram(own, plan, left, tiles):
    vmem = pl.BlockSpec(memory_space=pltpu.VMEM)
    smem = pl.BlockSpec(memory_space=pltpu.SMEM)
    widths = [
        TILE * (min(place + REACH, WIDE - 1) - max(place - REACH, 0) + 1) for place in range(WIDE)
    ]
    return pl.pallas_call(
        shared_kernel,
        out_shape=tuple(jax.ShapeDtypeStruct((TILE, width), jnp.float32) for width in widths),
        in_specs=[smem, smem, vmem, vmem],
        out_specs=(vmem,) * WIDE,
        scratch_shapes=[
            pltpu.VMEM((LANES, 2 * LANES), jnp.float32),
            pltpu.VMEM((WIDE * TILE - LANES, WIDE * TILE - LANES), jnp.float32),
        ],
        compiler_params=pltpu.CompilerParams(vmem_limit_bytes=32 * 1024 * 1024),
        name="shared_gram",
    )(own, plan, left, tiles)


def assemble(parts, shifts, count):
    total = None
    for place, (part, shift) in enumerate(zip(parts, shifts)):
        if shift:
            part = lax.ppermute(
                part, "row", [(device, (device + shift) % count) for device in range(count)]
            )
        before = max(REACH - place, 0) * TILE
        after = (2 * REACH + 1) * TILE - before - part.shape[1]
        part = jnp.pad(part, ((0, 0), (before, after)))
        total = part if total is None else total + part
    return total


def exchange(value):
    return lax.all_to_all(value, "row", split_axis=0, concat_axis=0, tiled=True)


def local_balanced(
    three_index, occupied_factor, virtual_factor, pair_list, occupancy, pair_blocks
):
    count = lax.axis_size("row")
    own = lax.axis_index("row")
    *packed, plan, level = source(
        three_index, virtual_factor, pair_list, occupancy, pair_blocks
    )
    own = own.reshape(1).astype(jnp.int32)

    def at_level(index):
        def run(packed):
            tiles = exchange(packed[index])
            left = left_factors(own, pair_blocks, occupied_factor)
            return shared_gram(own, plan, left, tiles)

        return run

    parts = lax.switch(level[0], [at_level(index) for index in range(len(packed))], packed)
    return assemble(parts, range(1 - SPAN, 2), count)


def local_padded(three_index, occupied_factor, virtual_factor, pair_list, occupancy, pair_blocks):
    count = lax.axis_size("row")
    own = lax.axis_index("row")
    packed = pack(three_index, pair_list, occupancy)
    tiles = exchange(packed)
    blocks = lax.dynamic_index_in_dim(pair_blocks, own, 0, keepdims=False)
    left, right = factors(blocks, occupied_factor, virtual_factor)
    parity = lax.rem(own, 2).reshape(1).astype(jnp.int32)
    parts = gram(parity, left, right, tiles)
    return assemble(parts, range(1 - SPAN, 1), count)


def local(three_index, *rest):
    whole_rows = three_index.shape[1] == ROWS
    return (local_balanced if whole_rows else local_padded)(three_index, *rest)


def solution(mesh):
    placed = (
        P(None, "row", "grp"),
        P("grp", None, None),
        P("grp", None, None),
        P("grp", None),
        P("grp"),
        P(),
    )
    return jax.shard_map(
        local, mesh=mesh, in_specs=placed, out_specs=P(("grp", "row"), None), check_vma=False
    )
```

```python
import functools

import jax
import jax.numpy as jnp
from jax import lax
from jax.experimental import pallas as pl
from jax.experimental.pallas import tpu as pltpu
from jax.sharding import PartitionSpec as P

TILE = 64
SPAN = 5
REACH = 2
LANES = 128
ROWS = 256
FOLD = ROWS // TILE


def pack_kernel(list_ref, occupancy_ref, source_ref, packed_ref):
    count, slots = list_ref.shape
    entries = source_ref.shape[1]
    low_half = lax.broadcasted_iota(jnp.int32, (1, LANES), 1) < TILE

    def pick(group, pair):
        slot = jnp.int32(0)
        found = jnp.int32(0)
        for j in range(slots):
            hit = (list_ref[group, j] == pair) & (j < occupancy_ref[group])
            slot = jnp.where(hit, j, slot)
            found = jnp.where(hit, 1, found)
        return slot, found

    def columns(group):
        return pl.ds(pl.multiple_of((group // 2) * LANES, LANES), LANES)

    def step(index, carry):
        for parity in range(2):
            pair = 2 * index + parity
            for couple in range(2):
                first = lax.rem(pair - 4 + 2 * couple + count, count)
                second = lax.rem(pair - 3 + 2 * couple + count, count)
                low, high = (first, second) if parity == 0 else (second, first)
                low_slot, low_found = pick(low, pair)
                high_slot, high_found = pick(high, pair)
                found = jnp.where(low_half, low_found, high_found) > 0
                value = jnp.where(
                    low_half,
                    source_ref[low_slot, :, columns(low)],
                    source_ref[high_slot, :, columns(high)],
                )
                packed_ref[pair, pl.ds(couple * entries, entries), :] = jnp.where(
                    found, value, jnp.zeros_like(value)
                )
            slot, found = pick(pair, pair)
            value = source_ref[slot, :, columns(pair)]
            value = jnp.where(found > 0, value, jnp.zeros_like(value))
            upper, under = value[: entries // 2], value[entries // 2 :]
            if parity == 0:
                folded = jnp.concatenate([upper[:, :TILE], under[:, :TILE]], axis=1)
            else:
                folded = jnp.concatenate([upper[:, TILE:], under[:, TILE:]], axis=1)
            packed_ref[pair, pl.ds(2 * entries, entries // 2), :] = folded
        return carry

    lax.fori_loop(0, count // 2, step, 0)


def pack(three_index, pair_list, occupancy):
    count = pair_list.shape[0]
    entries = three_index.shape[1]
    return pl.pallas_call(
        pack_kernel,
        out_shape=jax.ShapeDtypeStruct((count, 5 * entries // 2, LANES), jnp.bfloat16),
        in_specs=[
            pl.BlockSpec(memory_space=pltpu.SMEM),
            pl.BlockSpec(memory_space=pltpu.SMEM),
            pl.BlockSpec(memory_space=pltpu.VMEM),
        ],
        out_specs=pl.BlockSpec(memory_space=pltpu.VMEM),
        compiler_params=pltpu.CompilerParams(vmem_limit_bytes=32 * 1024 * 1024),
        name="pack",
    )(pair_list, occupancy, three_index)


def factor_kernel(index_ref, occupied_ref, virtual_ref, left_ref, right_ref):
    row = lax.broadcasted_iota(jnp.int32, (ROWS, ROWS), 0)
    column = lax.broadcasted_iota(jnp.int32, (ROWS, ROWS), 1)
    spread = (
        lax.broadcasted_iota(jnp.int32, (ROWS, TILE), 0) // FOLD
        == lax.broadcasted_iota(jnp.int32, (ROWS, TILE), 1)
    ).astype(jnp.bfloat16)
    block = lax.dot_general(
        spread, virtual_ref[0], (((1,), (1,)), ((), ())), preferred_element_type=jnp.float32
    )
    block = jnp.concatenate([block] * FOLD, axis=1)
    right_ref[...] = jnp.where(row % FOLD == column // TILE, block, 0.0).astype(jnp.bfloat16)
    entry = lax.broadcasted_iota(jnp.int32, (TILE, ROWS), 1)
    spread = (
        (entry // (FOLD * FOLD)) * FOLD + entry % FOLD
        == lax.broadcasted_iota(jnp.int32, (TILE, ROWS), 0)
    ).astype(jnp.bfloat16)
    block = lax.dot_general(
        occupied_ref[0], spread, (((0,), (0,)), ((), ())), preferred_element_type=jnp.float32
    )
    block = jnp.concatenate([block] * FOLD, axis=0)
    left_ref[...] = jnp.where(row // TILE == (column // FOLD) % FOLD, block, 0.0).astype(
        jnp.bfloat16
    )


def factors(blocks, occupied_factor, virtual_factor):
    shape = jax.ShapeDtypeStruct((ROWS, ROWS), jnp.bfloat16)
    whole = pl.BlockSpec((ROWS, ROWS), lambda i, index: (0, 0))
    return pl.pallas_call(
        factor_kernel,
        out_shape=(shape, shape),
        grid_spec=pltpu.PrefetchScalarGridSpec(
            num_scalar_prefetch=1,
            grid=(1,),
            in_specs=[
                pl.BlockSpec((1, TILE, TILE), lambda i, index: (index[0], 0, 0)),
                pl.BlockSpec((1, TILE, TILE), lambda i, index: (index[1], 0, 0)),
            ],
            out_specs=(whole, whole),
        ),
        cost_estimate=pl.CostEstimate(
            flops=4_000_000, bytes_accessed=300_000, transcendentals=0
        ),
        name="factors",
    )(blocks, occupied_factor, virtual_factor)


def gram_kernel(parity_ref, left_ref, right_ref, tiles_ref, *refs):
    outs, half_ref, gram_ref = refs[:SPAN], refs[SPAN], refs[SPAN + 1]
    entries = tiles_ref.shape[1] * 2 // 5
    sources = ROWS // entries
    steps = ROWS // (FOLD * FOLD)
    for block in range(TILE * TILE // ROWS):
        span = pl.ds(block * sources, sources)
        first = tiles_ref[span, pl.ds(0, entries), :].reshape(ROWS, LANES)
        second = tiles_ref[span, pl.ds(entries, entries), :].reshape(ROWS, LANES)
        third = tiles_ref[span, pl.ds(2 * entries, entries // 2), :]
        third = jnp.concatenate([third[..., :TILE], third[..., TILE:]], axis=1)
        values = jnp.concatenate([first, second, third.reshape(ROWS, TILE)], axis=1)
        half = jnp.dot(right_ref[...], values, preferred_element_type=jnp.float32)
        half_ref[block] = half.astype(jnp.bfloat16).reshape(steps, FOLD * FOLD, SPAN * TILE)
    for step in range(steps):
        values = half_ref[:, step].reshape(ROWS, SPAN * TILE)
        panel = jnp.dot(left_ref[...], values, preferred_element_type=jnp.float32)
        panel = panel.astype(jnp.bfloat16)
        part = lax.dot_general(
            panel, panel, (((0,), (0,)), ((), ())), preferred_element_type=jnp.float32
        )
        if step == 0:
            gram_ref[...] = part
        else:
            gram_ref[...] += part
    odd = parity_ref[0] == 1
    scale = 0.5 / TILE
    for place in range(SPAN):
        swapped = place ^ 1 if place < SPAN - 1 else place
        rows = jnp.where(
            odd,
            gram_ref[pl.ds(swapped * TILE, TILE), :],
            gram_ref[pl.ds(place * TILE, TILE), :],
        )
        rows = rows * scale
        pieces = []
        for other in range(max(place - REACH, 0), min(place + REACH, SPAN - 1) + 1):
            turned = other ^ 1 if other < SPAN - 1 else other
            pieces.append(
                jnp.where(
                    odd,
                    rows[:, turned * TILE : (turned + 1) * TILE],
                    rows[:, other * TILE : (other + 1) * TILE],
                )
            )
        outs[place][...] = jnp.concatenate(pieces, axis=1)


def neighbours(place):
    return min(place + REACH, SPAN - 1) - max(place - REACH, 0) + 1


def gram(parity, left, right, tiles):
    vmem = pl.BlockSpec(memory_space=pltpu.VMEM)
    return pl.pallas_call(
        gram_kernel,
        out_shape=tuple(
            jax.ShapeDtypeStruct((TILE, TILE * neighbours(place)), jnp.float32)
            for place in range(SPAN)
        ),
        in_specs=[pl.BlockSpec(memory_space=pltpu.SMEM), vmem, vmem, vmem],
        out_specs=(vmem,) * SPAN,
        scratch_shapes=[
            pltpu.VMEM((TILE * TILE // ROWS, ROWS // (FOLD * FOLD), FOLD * FOLD, SPAN * TILE), jnp.bfloat16),
            pltpu.VMEM((SPAN * TILE, SPAN * TILE), jnp.float32),
        ],
        compiler_params=pltpu.CompilerParams(vmem_limit_bytes=32 * 1024 * 1024),
        name="gram",
    )(parity, left, right, tiles)


CHUNKS = 8
WRAP = 6
BATCH = 2
CAPACITIES = (26, 28, 30, 36)
ROOM = CAPACITIES[-1]
UNIT = FOLD * FOLD
RECIPROCALS = (4096, 2048, 1366, 1024, 820)


def swap_halves(value):
    return jnp.concatenate([value[:, TILE:], value[:, :TILE]], axis=1)


def plan_tiles(list_ref, occupancy_ref, plan_ref, level_ref):
    slots, count = list_ref.shape
    held, shed = SPAN * count, SPAN * count + count

    for index in range(SPAN * count):
        plan_ref[index] = 0
    for group in range(count):
        for j in range(slots):
            t = list_ref[j, group] - group
            t = jnp.where(t < 0, t + count, t)
            plan_ref[group * SPAN + t] = jnp.where(j < occupancy_ref[group], j + 1, -1)
    entries = [[plan_ref[group * SPAN + t] for t in range(SPAN)] for group in range(count)]

    def quotient(value, factor):
        return (value * factor) >> 12

    heres, factors = [], []
    for pair in range(count):
        here = jnp.int32(0)
        for t in range(SPAN):
            here += jnp.where(entries[(pair - t) % count][t] > 0, 1, 0)
        factor = jnp.int32(RECIPROCALS[-1])
        for d in range(SPAN - 1, 0, -1):
            factor = jnp.where(here <= d, RECIPROCALS[d - 1], factor)
        heres.append(here)
        factors.append(jnp.where(here > 0, factor, 0))
        plan_ref[held + pair] = here
    def shares(capacity):
        gives = [None] * count
        taken = jnp.int32(0)
        again = range(count - 1, count - 1 - WRAP, -1)
        for pair in (*range(count - 1, -1, -1), *again):
            here = heres[pair]
            excess = jnp.maximum(CHUNKS * here - capacity + taken, 0)
            gives[pair] = jnp.minimum(quotient(excess + here - 1, factors[pair]), CHUNKS)
            taken = here * gives[pair]
        most = jnp.int32(0)
        for pair in range(count):
            after = (pair + 1) % count
            load = heres[pair] * (CHUNKS - gives[pair]) + heres[after] * gives[after]
            most = jnp.maximum(most, load)
        return gives, most <= capacity

    level = jnp.int32(len(CAPACITIES) - 1)
    gives = [jnp.int32(0)] * count
    for index in range(len(CAPACITIES) - 2, -1, -1):
        tried, fits = shares(CAPACITIES[index])
        level = jnp.where(fits, index, level)
        gives = [jnp.where(fits, new, old) for new, old in zip(tried, gives)]
    for pair in range(count):
        plan_ref[shed + pair] = gives[pair]
    level_ref[0] = level

    @pl.when(level == len(CAPACITIES) - 1)
    def _():
        for pair in range(count):
            listed = jnp.int32(0)
            before = jnp.int32(0)
            for t in range(SPAN):
                listed += jnp.where(entries[(pair - t) % count][t] != 0, 1, 0)
            for distance in range(1, SPAN):
                for t in range(distance):
                    before += jnp.where(entries[(pair - distance) % count][t] != 0, 1, 0)
            factor = jnp.int32(RECIPROCALS[-1])
            for d in range(SPAN - 1, 0, -1):
                factor = jnp.where(listed <= d, RECIPROCALS[d - 1], factor)
            give = quotient(CHUNKS * (2 * SPAN - before), factor)
            plan_ref[shed + pair] = jnp.where(listed > 0, give, 0)

    return entries, heres


def source_kernel(
    list_hbm, occupancy_hbm, blocks_hbm, tiles_hbm, virtual_hbm,
    *refs,
):
    outs, refs = refs[: len(CAPACITIES)], refs[len(CAPACITIES) :]
    plan_ref, level_ref, list_ref, occupancy_ref, blocks_ref, *refs = refs
    tiles_ref, virtual_ref, right_ref, packed_ref, small_sem, virtual_sem, in_sem, out_sem = refs
    count = list_ref.shape[1]
    shed = SPAN * count + count
    parts = count // 8
    width = 8 * TILE
    small = [
        pltpu.make_async_copy(there, here, small_sem.at[index])
        for index, (there, here) in enumerate(
            ((blocks_hbm, blocks_ref), (list_hbm, list_ref), (occupancy_hbm, occupancy_ref))
        )
    ]
    for copy in small:
        copy.start()
    fetches = []
    for part in range(parts):
        lanes = pl.ds(part * width, width)
        fetches.append(
            pltpu.make_async_copy(
                tiles_hbm.at[:, :, lanes], tiles_ref.at[:, :, lanes], in_sem.at[part]
            )
        )
    table = pltpu.make_async_copy(virtual_hbm, virtual_ref, virtual_sem.at[0])
    table.start()
    for copy in fetches:
        copy.start()
    small[0].wait()
    small[1].wait()
    small[2].wait()
    table.wait()
    low = lax.broadcasted_iota(jnp.int32, (1, LANES), 1) < TILE
    spread = (
        lax.broadcasted_iota(jnp.int32, (ROWS, TILE), 0) // FOLD
        == lax.broadcasted_iota(jnp.int32, (ROWS, TILE), 1)
    ).astype(jnp.bfloat16)
    diagonal = (
        lax.broadcasted_iota(jnp.int32, (ROWS, ROWS), 0) % FOLD
        == lax.broadcasted_iota(jnp.int32, (ROWS, ROWS), 1) // TILE
    ).astype(jnp.bfloat16)
    for couple in range(0, count, 2):
        chosen = [virtual_ref[blocks_ref[1, couple + side]] for side in range(2)]
        block = lax.dot_general(
            spread,
            jnp.concatenate(chosen, axis=0),
            (((1,), (1,)), ((), ())),
            preferred_element_type=jnp.float32,
        ).astype(jnp.bfloat16)
        turned = swap_halves(block)
        for side in range(2):
            double = jnp.where(low, turned, block) if side else jnp.where(low, block, turned)
            right_ref[couple + side] = jnp.concatenate([double, double], axis=1) * diagonal
    entries, heres = plan_tiles(list_ref, occupancy_ref, plan_ref, level_ref)
    gives = [plan_ref[shed + pair] for pair in range(count)]
    level = level_ref[0]

    def send(dests, act):
        for index, capacity in enumerate(CAPACITIES):

            @pl.when(level == index)
            def _(index=index, capacity=capacity):
                for dest in dests:
                    held = packed_ref.at[pl.ds(dest * (ROOM + 1), capacity)]
                    copy = pltpu.make_async_copy(held, outs[index].at[dest], out_sem.at[dest])
                    copy.start() if act else copy.wait()

    arrived = set()
    written = set()
    sent = []
    started = 0
    for index in range(count):
        pair = (index + 4) % count
        previous = (pair - 1) % count
        for t in range(SPAN):
            part = ((pair - t) % count) // 8
            if part not in arrived:
                arrived.add(part)
                fetches[part].wait()
        values, ranks = [], []
        rank = jnp.int32(0)
        for place in range(SPAN):
            t = SPAN - 1 - place
            group = (pair - t) % count
            entry = entries[group][t]
            columns = pl.ds((group // 2) * LANES, LANES)
            values.append(tiles_ref[jnp.maximum(entry - 1, 0), :, columns])
            ranks.append((entry > 0, rank))
            rank += jnp.where(entry > 0, 1, 0)
        parity = pair % 2
        lows = [values[place] for place in range(parity, SPAN, 2)]
        highs = [values[place] for place in range(1 - parity, SPAN, 2)]
        if parity == 0:
            highs.append(lows[-1])
        else:
            lows.append(highs[-1])
        joined = [jnp.where(low, a, b) for a, b in zip(lows, highs)]
        half = jnp.dot(
            right_ref[pair], jnp.concatenate(joined, axis=1), preferred_element_type=jnp.float32
        ).astype(jnp.bfloat16)
        here, give = heres[pair], gives[pair]
        base = previous * (ROOM + 1) + heres[previous] * (CHUNKS - gives[previous])
        starts = []
        for chunk in range(CHUNKS):
            starts.append(
                jnp.where(
                    chunk >= give,
                    pair * (ROOM + 1) + (chunk - give) * here,
                    base + chunk * here,
                )
            )
        middle = ROWS // 2
        for place in range(SPAN):
            piece = half[:, (place // 2) * LANES : (place // 2 + 1) * LANES]
            if (place + parity) % 2 == 0:
                folded = jnp.where(low, piece[:middle], swap_halves(piece[middle:]))
            else:
                folded = jnp.where(low, swap_halves(piece[:middle]), piece[middle:])
            found, rank = ranks[place]
            for chunk in range(CHUNKS):
                slot = jnp.where(found, starts[chunk] + rank, count * (ROOM + 1))
                packed_ref[slot] = folded[chunk * UNIT : (chunk + 1) * UNIT]
        written.add(pair)
        for dest in (pair, previous):
            if dest in written and (dest + 1) % count in written and dest not in sent:
                sent.append(dest)
        if index % BATCH == BATCH - 1:
            send(sent[started:], True)
            started = len(sent)
    send(sent, False)


def source(three_index, virtual_factor, pair_list, occupancy, pair_blocks):
    count = pair_list.shape[0]
    smem = pl.BlockSpec(memory_space=pltpu.SMEM)
    hbm = pl.BlockSpec(memory_space=pltpu.HBM)
    return pl.pallas_call(
        source_kernel,
        out_shape=(
            *(
                jax.ShapeDtypeStruct((count, capacity, UNIT, LANES), jnp.bfloat16)
                for capacity in CAPACITIES
            ),
            jax.ShapeDtypeStruct(((SPAN + 2) * count,), jnp.int32),
            jax.ShapeDtypeStruct((1,), jnp.int32),
        ),
        in_specs=[hbm] * 5,
        out_specs=(hbm,) * len(CAPACITIES) + (smem, smem),
        scratch_shapes=[
            pltpu.SMEM(pair_list.shape[::-1], jnp.int32),
            pltpu.SMEM(occupancy.shape, jnp.int32),
            pltpu.SMEM(pair_blocks.shape[::-1], jnp.int32),
            pltpu.VMEM(three_index.shape, jnp.bfloat16),
            pltpu.VMEM(virtual_factor.shape, jnp.bfloat16),
            pltpu.VMEM((count, ROWS, ROWS), jnp.bfloat16),
            pltpu.VMEM((count * (ROOM + 1) + 1, UNIT, LANES), jnp.bfloat16),
            pltpu.SemaphoreType.DMA((3,)),
            pltpu.SemaphoreType.DMA((1,)),
            pltpu.SemaphoreType.DMA((count // 4,)),
            pltpu.SemaphoreType.DMA((count,)),
        ],
        compiler_params=pltpu.CompilerParams(vmem_limit_bytes=60 * 1024 * 1024),
        name="source",
    )(pair_list.T, occupancy, pair_blocks.T, three_index, virtual_factor)


def left_kernel(own_ref, blocks_hbm, occupied_hbm, left_ref, blocks_ref, occupied_ref, sem):
    count = blocks_ref.shape[1]
    fetch = pltpu.make_async_copy(blocks_hbm, blocks_ref, sem.at[0])
    fetch.start()
    fetch.wait()
    copies = []
    for segment in range(2):
        pair = own_ref[0] + segment
        pair = jnp.where(pair >= count, pair - count, pair)
        copies.append(
            pltpu.make_async_copy(
                occupied_hbm.at[blocks_ref[0, pair]], occupied_ref.at[segment], sem.at[segment + 1]
            )
        )
        copies[-1].start()
    row = lax.broadcasted_iota(jnp.int32, (ROWS, ROWS), 0)
    column = lax.broadcasted_iota(jnp.int32, (ROWS, ROWS), 1)
    entry = lax.broadcasted_iota(jnp.int32, (TILE, ROWS), 1)
    spread = (
        (entry // UNIT) * FOLD + entry % FOLD
        == lax.broadcasted_iota(jnp.int32, (TILE, ROWS), 0)
    ).astype(jnp.bfloat16)
    for segment in range(2):
        copies[segment].wait()
        block = lax.dot_general(
            occupied_ref[segment],
            spread,
            (((0,), (0,)), ((), ())),
            preferred_element_type=jnp.float32,
        )
        block = jnp.concatenate([block] * FOLD, axis=0)
        left_ref[segment] = jnp.where(
            row // TILE == (column // FOLD) % FOLD, block, 0.0
        ).astype(jnp.bfloat16)


def left_factors(own, pair_blocks, occupied_factor):
    hbm = pl.BlockSpec(memory_space=pltpu.HBM)
    return pl.pallas_call(
        left_kernel,
        out_shape=jax.ShapeDtypeStruct((2, ROWS, ROWS), jnp.bfloat16),
        in_specs=[pl.BlockSpec(memory_space=pltpu.SMEM), hbm, hbm],
        out_specs=pl.BlockSpec(memory_space=pltpu.VMEM),
        scratch_shapes=[
            pltpu.SMEM(pair_blocks.shape[::-1], jnp.int32),
            pltpu.VMEM((2,) + occupied_factor.shape[1:], jnp.bfloat16),
            pltpu.SemaphoreType.DMA((3,)),
        ],
        cost_estimate=pl.CostEstimate(
            flops=4_000_000, bytes_accessed=300_000, transcendentals=0
        ),
        compiler_params=pltpu.CompilerParams(vmem_limit_bytes=16 * 1024 * 1024),
        name="left_factors",
    )(own, pair_blocks.T, occupied_factor)


WIDE = SPAN + 1
UNROLL = 3


def shared_kernel(own_ref, plan_ref, left_ref, tiles_ref, *refs):
    outs, first_ref, rest_ref = refs[:WIDE], refs[WIDE], refs[WIDE + 1]
    count, capacity = tiles_ref.shape[:2]
    held, shed = SPAN * count, SPAN * count + count
    own = own_ref[0]
    after = jnp.where(own == count - 1, 0, own + 1)
    rows_with_rows = (((1,), (1,)), ((), ()))
    first_ref[...] = jnp.zeros_like(first_ref)
    rest_ref[...] = jnp.zeros_like(rest_ref)

    def tiles_of(pair, shift):
        found, ranks = [False] * WIDE, [0] * WIDE
        rank = jnp.int32(0)
        for place in range(SPAN):
            t = SPAN - 1 - place
            group = pair - t
            group = jnp.where(group < 0, group + count, group)
            found[place + shift] = plan_ref[group * SPAN + t] > 0
            ranks[place + shift] = rank
            rank += jnp.where(found[place + shift], 1, 0)
        return found, ranks

    own_here, after_here = plan_ref[held + own], plan_ref[held + after]
    own_units = CHUNKS - plan_ref[shed + own]
    units = own_units + plan_ref[shed + after]
    own_found, own_ranks = tiles_of(own, 0)
    after_found, after_ranks = tiles_of(after, 1)

    def gather(index):
        second = index >= own_units
        here = jnp.where(second, after_here, own_here)
        base = jnp.where(second, own_units * own_here, 0)
        base += jnp.where(second, index - own_units, index) * here
        values = []
        for place in range(WIDE):
            found = jnp.where(second, after_found[place], own_found[place])
            found = found & (index < units)
            slot = base + jnp.where(second, after_ranks[place], own_ranks[place])
            slot = jnp.where(found, slot, 0)
            value = tiles_ref[:, jnp.minimum(slot, capacity - 1)]
            value = jnp.where(found, value, jnp.zeros_like(value))
            values.append(value.reshape(ROWS, LANES))
        return lax.dot_general(
            jnp.concatenate(values, axis=1).T,
            left_ref[jnp.where(second, 1, 0)],
            rows_with_rows,
            preferred_element_type=jnp.float32,
        ).astype(jnp.bfloat16)

    def step(index, carry):
        for inner in range(UNROLL):
            panel = gather(UNROLL * index + inner).reshape(WIDE, 2, TILE, ROWS)
            stack = jnp.concatenate(
                [panel[:, half].reshape(WIDE * TILE, ROWS) for half in range(2)], axis=1
            )
            first_ref[...] += lax.dot_general(
                stack[:LANES], stack[: 2 * LANES], rows_with_rows, preferred_element_type=jnp.float32
            )
            rest = stack[LANES:]
            rest_ref[...] += lax.dot_general(
                rest, rest, rows_with_rows, preferred_element_type=jnp.float32
            )
        return carry

    lax.fori_loop(0, (units + UNROLL - 1) // UNROLL, step, 0)

    turned = first_ref[:, LANES:].T
    scale = 0.5 / TILE
    for place in range(WIDE):
        if place < 2:
            rows = first_ref[pl.ds(place * TILE, TILE), :]
        else:
            rows = rest_ref[pl.ds((place - 2) * TILE, TILE), :]
            left = turned[(place - 2) * TILE : (place - 1) * TILE] if place < 4 else rows[:, :LANES]
            rows = jnp.concatenate([left, rows], axis=1)
        first, last = max(place - REACH, 0), min(place + REACH, WIDE - 1)
        outs[place][...] = rows[:, first * TILE : (last + 1) * TILE] * scale


def shared_gram(own, plan, left, tiles):
    vmem = pl.BlockSpec(memory_space=pltpu.VMEM)
    smem = pl.BlockSpec(memory_space=pltpu.SMEM)
    widths = [
        TILE * (min(place + REACH, WIDE - 1) - max(place - REACH, 0) + 1) for place in range(WIDE)
    ]
    return pl.pallas_call(
        shared_kernel,
        out_shape=tuple(jax.ShapeDtypeStruct((TILE, width), jnp.float32) for width in widths),
        in_specs=[smem, smem, vmem, vmem],
        out_specs=(vmem,) * WIDE,
        scratch_shapes=[
            pltpu.VMEM((LANES, 2 * LANES), jnp.float32),
            pltpu.VMEM((WIDE * TILE - LANES, WIDE * TILE - LANES), jnp.float32),
        ],
        compiler_params=pltpu.CompilerParams(vmem_limit_bytes=32 * 1024 * 1024),
        name="shared_gram",
    )(own, plan, left, tiles)


def assemble(parts, shifts, count):
    total = None
    for place, (part, shift) in enumerate(zip(parts, shifts)):
        if shift:
            part = lax.ppermute(
                part, "row", [(device, (device + shift) % count) for device in range(count)]
            )
        before = max(REACH - place, 0) * TILE
        after = (2 * REACH + 1) * TILE - before - part.shape[1]
        part = jnp.pad(part, ((0, 0), (before, after)))
        total = part if total is None else total + part
    return total


def exchange(value):
    return lax.all_to_all(value, "row", split_axis=0, concat_axis=0, tiled=True)


def local_balanced(
    three_index, occupied_factor, virtual_factor, pair_list, occupancy, pair_blocks
):
    count = lax.axis_size("row")
    own = lax.axis_index("row")
    *packed, plan, level = source(
        three_index, virtual_factor, pair_list, occupancy, pair_blocks
    )
    own = own.reshape(1).astype(jnp.int32)

    def at_level(index):
        def run(packed):
            tiles = exchange(packed[index])
            left = left_factors(own, pair_blocks, occupied_factor)
            return shared_gram(own, plan, left, tiles)

        return run

    parts = lax.switch(level[0], [at_level(index) for index in range(len(packed))], packed)
    return assemble(parts, range(1 - SPAN, 2), count)


def local_padded(three_index, occupied_factor, virtual_factor, pair_list, occupancy, pair_blocks):
    count = lax.axis_size("row")
    own = lax.axis_index("row")
    packed = pack(three_index, pair_list, occupancy)
    tiles = exchange(packed)
    blocks = lax.dynamic_index_in_dim(pair_blocks, own, 0, keepdims=False)
    left, right = factors(blocks, occupied_factor, virtual_factor)
    parity = lax.rem(own, 2).reshape(1).astype(jnp.int32)
    parts = gram(parity, left, right, tiles)
    return assemble(parts, range(1 - SPAN, 1), count)


def local(three_index, *rest):
    whole_rows = three_index.shape[1] == ROWS
    return (local_balanced if whole_rows else local_padded)(three_index, *rest)


def solution(mesh):
    placed = (
        P(None, "row", "grp"),
        P("grp", None, None),
        P("grp", None, None),
        P("grp", None),
        P("grp"),
        P(),
    )
    return jax.shard_map(
        local, mesh=mesh, in_specs=placed, out_specs=P(("grp", "row"), None), check_vma=False
    )
```
